512 devices in a mesh: expert: 8 (over y, core), tensor: 64 (over x, z).
Axes of the slice: x: 4, y: 4, z: 16, core: 2. Of those that a mesh axis runs over, the one named last changes fastest.
Arguments:
- tokens: bfloat16 [1024, 2048], P('expert', 'tensor'), may hold values from -6 to 6
- out_grad: bfloat16 [1024, 2048], P('expert', 'tensor'), may hold values from -3 to 3
- routes: int32 [1024, 2], P('expert'), may hold values from 0 to 7, all different within a row; in each aligned block of 128 rows (0 to 127, 128 to 255, ...) at most 64 rows name the same one
- gate_values: bfloat16 [1024, 2], P('expert'), may hold values from 0.049804688 to 0.94921875
- gate_weight: bfloat16 [8, 2048, 8192], P('expert', None, 'tensor'), may hold values from -0.125 to 0.125
- up_weight: bfloat16 [8, 2048, 8192], P('expert', None, 'tensor'), may hold values from -0.125 to 0.125
- down_weight: bfloat16 [8, 8192, 2048], P('expert', 'tensor'), may hold values from -0.0625 to 0.0625
Outputs:
- tokens_grad: bfloat16 [1024, 2048], P('expert', 'tensor')
- gate_values_grad: float32 [1024, 2], P('expert')
- gate_weight_grad: bfloat16 [8, 2048, 8192], P('expert', None, 'tensor')
- up_weight_grad: bfloat16 [8, 2048, 8192], P('expert', None, 'tensor')
- down_weight_grad: bfloat16 [8, 8192, 2048], P('expert', 'tensor')
The draws below stay inside these ranges and needn't reach their ends.
Inputs may be any that keep to these rules, and one draw needn't show every extreme that they name: `routes`: each token names 2 different experts. Among the 128 tokens of one index of the expert axis no expert is named by more than 64 of them, and in some such block one expert is named by exactly 64.
All inputs are finite; a program needn't handle non-finite values.
Results may differ from the reference program's by a relative error of at most 0.005.
Values may be sent and summed in bfloat16 or wider, within the bound.
A program may use at most 64 MiB of HBM per device.

```python
import math
import jax
import jax.numpy as jnp
import numpy as np
from jax import lax

D = 2048
FF = 8192
TOP = 2
TOK_GRP = 128
EXPERTS = 8
CAP = 64
TOKENS = 1024


def level_of(own_key, dims, pieces, low, high):
    level, own = 1.0, jax.random.fold_in(own_key, 6)
    for position, shards_of in pieces:
        steps = jnp.exp(jax.random.uniform(jax.random.fold_in(own, position), (shards_of,), jnp.float32, low / len(pieces), high / len(pieces)))
        level = level * jnp.repeat(steps, dims[position] // shards_of).reshape([-1 if axis == position else 1 for axis in range(len(dims))])
    return level


def deal_out(stream_key, own, number, rows, count, top, most, skew):
    sequence = jax.random.permutation(stream_key, count)
    heavy_load, ordinary = load_shares(count, rows * top, most, skew, True), load_shares(count, rows * top, most, skew, False)
    places = jnp.arange(count)

    def named(lengths, rotation):
        used = int((lengths > 0).sum())
        fixed = max(1, used // 4)
        passed = fixed + (places - fixed + rotation * (used - fixed)) % max(1, count - fixed)
        return jnp.zeros((count,), jnp.int32).at[sequence[jnp.where(places < fixed, places, passed)]].set(jnp.asarray(lengths, jnp.int32))

    lengths = jnp.where(number % 4 == 0, named(heavy_load, number // 4), named(ordinary, number - number // 4 - 1))
    mixed = jax.random.permutation(jax.random.fold_in(own, 3), count)
    donor, receiver = mixed[0:count // 2 * 2:2], mixed[1:count // 2 * 2:2]
    room = jnp.minimum(lengths[donor] - 1, most - lengths[receiver]) // 2
    room = jnp.where((donor == sequence[0]) | (receiver == sequence[0]) | (lengths[receiver] == 0), 0, jnp.maximum(room, 0))
    passed = jax.random.randint(jax.random.fold_in(own, 4), (count // 2,), 0, 1 << 20) % (room + 1)
    lengths = lengths.at[donor].add(-passed).at[receiver].add(passed)
    members = jnp.searchsorted(jnp.cumsum(lengths), jnp.arange(rows * top), side="right").astype(jnp.int32)
    listing = members.reshape(top, rows).T
    listing = listing[jax.random.permutation(jax.random.fold_in(own, 1), rows)]
    rotation = jax.random.randint(jax.random.fold_in(own, 2), (rows, 1), 0, top)
    return jnp.take_along_axis(listing, (jnp.arange(top)[None, :] + rotation) % top, axis=1)


def load_shares(count, total, bound, lean, full):
    loads = [(1 << 20) // math.isqrt(grade ** lean) + 1 for grade in range(1, count + 1)]
    largest = bound if full else min(bound, max(-(-total // count), total * loads[0] // sum(loads)))
    least = 1 if total - largest >= count - 1 else 0
    given, surplus = [largest] + [least] * (count - 1), total - largest - least * (count - 1)
    while surplus > 0:
        candidates = [i for i in range(1, count) if given[i] < largest] or [i for i in range(1, count) if given[i] < bound]
        pool, remaining = sum([loads[i] for i in candidates]), surplus
        for i in candidates:
            extra = min(bound - given[i], max(1, remaining * loads[i] // pool), surplus)
            given[i] = given[i] + extra
            surplus = surplus - extra
    return np.array(given)


def noise(own_key, dims, deviation, most, pieces=(), dtype=jnp.bfloat16):
    gain = level_of(own_key, dims, pieces, -0.22, 0.18) if pieces else 1.0
    values = jax.random.normal(own_key, dims, jnp.float32) * deviation * gain
    return jnp.minimum(jnp.maximum(values, -most), most).astype(dtype)


def setup_inputs(seed: int = 0) -> dict:
    key_of = jax.random.split(jax.random.key(seed), 8)
    tokens = noise(key_of[0], (TOKENS, D), 1.0, 6.0, ((0, 8), (1, 64)))
    out_grad = noise(key_of[1], (TOKENS, D), 0.5, 3.0, ((0, 8), (1, 64)))
    routes_keys = jax.random.split(jax.random.fold_in(key_of[2], 1), TOKENS // TOK_GRP)
    routes_turns = jax.random.permutation(jax.random.fold_in(key_of[2], 3), TOKENS // TOK_GRP)
    routes = jax.vmap(lambda own, number: deal_out(jax.random.fold_in(key_of[2], 2), own, number, TOK_GRP, EXPERTS, TOP, CAP, 2))(routes_keys, routes_turns).reshape((TOKENS, TOP))
    gate_values = jnp.clip(0.049804688 + 0.89941406 * jax.random.uniform(key_of[3], (TOKENS, TOP), jnp.float32) ** level_of(key_of[3], (TOKENS, TOP), ((0, 8),), -0.2, 0.2), 0.049804688, 0.94921875).astype(jnp.bfloat16)
    gate_weight = noise(key_of[4], (EXPERTS, D, FF), D ** -0.5, 0.125, ((0, 8), (2, 64)))
    up_weight = noise(key_of[5], (EXPERTS, D, FF), D ** -0.5, 0.125, ((0, 8), (2, 64)))
    down_weight = noise(key_of[6], (EXPERTS, FF, D), FF ** -0.5, 0.0625, ((0, 8), (1, 64)))
    return {"tokens": tokens, "out_grad": out_grad, "routes": routes, "gate_values": gate_values, "gate_weight": gate_weight, "up_weight": up_weight, "down_weight": down_weight}


def silu_parts(pre_gate):
    sigmoid_gate = jax.nn.sigmoid(pre_gate)
    activated = pre_gate * sigmoid_gate
    slope = sigmoid_gate * (1.0 + pre_gate * (1.0 - sigmoid_gate))
    return activated, slope


def expert_backward(rows_in, grads_in, weights, gate_local, up_local, down_local):
    pre_gate = jnp.dot(rows_in, gate_local, preferred_element_type=jnp.float32)
    pre_up = jnp.dot(rows_in, up_local, preferred_element_type=jnp.float32)
    hidden_grad = lax.dot_general(grads_in, down_local, (((1,), (1,)), ((), ())), preferred_element_type=jnp.float32)
    activated, slope = silu_parts(pre_gate)
    gate_partial = jnp.sum(activated * pre_up * hidden_grad, axis=1)
    scaled_hidden = (weights[:, None] * activated * pre_up).astype(jnp.bfloat16)
    gate_pre_grad = (weights[:, None] * hidden_grad * pre_up * slope).astype(jnp.bfloat16)
    up_pre_grad = (weights[:, None] * hidden_grad * activated).astype(jnp.bfloat16)
    return gate_partial, scaled_hidden, gate_pre_grad, up_pre_grad


def reference(tokens, out_grad, routes, gate_values, gate_weight, up_weight, down_weight):
    rows_most = EXPERTS * CAP
    flat_routes = routes.reshape(-1)
    flat_values = gate_values.reshape(-1).astype(jnp.float32)
    input_total = jnp.zeros((TOKENS, D), jnp.float32)
    value_total = jnp.zeros((TOKENS * TOP,), jnp.float32)
    gate_grads = []
    up_grads = []
    down_grads = []
    for expert in range(EXPERTS):
        hit_mask = (flat_routes == expert).astype(jnp.int32)
        ordering = jnp.argsort(1 - hit_mask, stable=True)[:rows_most].astype(jnp.int32)
        taken_mask = hit_mask[ordering].astype(jnp.float32)
        token_ids = (ordering // TOP).astype(jnp.int32)
        rows_in = tokens[token_ids]
        grads_in = out_grad[token_ids]
        weights = flat_values[ordering] * taken_mask
        gate_partial, scaled_hidden, gate_pre_grad, up_pre_grad = expert_backward(
            rows_in, grads_in, weights, gate_weight[expert], up_weight[expert], down_weight[expert])
        value_total = value_total.at[ordering].add(gate_partial * taken_mask)
        input_rows = lax.dot_general(gate_pre_grad, gate_weight[expert], (((1,), (1,)), ((), ())), preferred_element_type=jnp.float32)
        input_rows = input_rows + lax.dot_general(up_pre_grad, up_weight[expert], (((1,), (1,)), ((), ())), preferred_element_type=jnp.float32)
        input_total = input_total.at[token_ids].add(input_rows * taken_mask[:, None])
        gate_grads.append(lax.dot_general(rows_in, gate_pre_grad, (((0,), (0,)), ((), ())), preferred_element_type=jnp.float32).astype(jnp.bfloat16))
        up_grads.append(lax.dot_general(rows_in, up_pre_grad, (((0,), (0,)), ((), ())), preferred_element_type=jnp.float32).astype(jnp.bfloat16))
        down_grads.append(lax.dot_general(scaled_hidden, grads_in, (((0,), (0,)), ((), ())), preferred_element_type=jnp.float32).astype(jnp.bfloat16))
    return (input_total.astype(jnp.bfloat16), value_total.reshape(TOKENS, TOP),
            jnp.stack(gate_grads), jnp.stack(up_grads), jnp.stack(down_grads))
```

```python
import functools

import jax
import jax.numpy as jnp
from jax import lax
from jax.experimental import pallas as pl
from jax.experimental.pallas import tpu as pltpu
from jax.sharding import PartitionSpec as P

MESH = pl.DeviceIdType.MESH
NX = 4
contract_cols = (((1,), (1,)), ((), ()))


def cols_to_row(ref, column, count):
    rows = lax.broadcasted_iota(jnp.int32, (count, count), 0)
    cols = lax.broadcasted_iota(jnp.int32, (count, count), 1)
    values = ref[:, column : column + 1].astype(jnp.float32)
    return jnp.sum(jnp.where(rows == cols, values, 0.0), axis=0, keepdims=True)


def row_to_col(row, count):
    rows = lax.broadcasted_iota(jnp.int32, (count, count), 0)
    cols = lax.broadcasted_iota(jnp.int32, (count, count), 1)
    return jnp.sum(jnp.where(rows == cols, row, 0.0), axis=1, keepdims=True)


def kernel(
    dims,
    tok_ref, grad_ref, routes_ref, values_ref, gate_hbm, up_hbm, down_hbm,
    tgrad_ref, vgrad_ref, ggrad_hbm, ugrad_hbm, dgrad_hbm,
    xt, gt, meta, wg, wu, wd, wt, ab, hh, own, sib_out, sib_in, s1, r1a, r1b,
    s2a, s2b, s2fa, s2fb, r2a, r2b, s3, s3f, r3, vp, vr, v1, vx, vz,
    og, ou, od, stage_t, stage_g, send_sems, recv_sems, local_sems,
):
    ny, nz, feat, tokens, hidden = dims
    e = lax.axis_index("expert")
    t = lax.axis_index("tensor")
    y, c = e // 2, e % 2
    x, z = t // nz, t % nz
    slab = nz * feat
    half_slab = slab // 2
    depth = NX * slab
    groups = 2 * ny

    counter = [0]
    pending = []

    def dev(xx=None, yy=None, zz=None, cc=None):
        xx = x if xx is None else xx
        yy = y if yy is None else yy
        zz = z if zz is None else zz
        cc = c if cc is None else cc
        return (yy * 2 + cc, xx * nz + zz)

    def take(count=1):
        first = counter[0]
        counter[0] += count
        return first

    def remote(src, dst, index, device):
        return pltpu.make_async_remote_copy(
            src_ref=src, dst_ref=dst, send_sem=send_sems.at[index], recv_sem=recv_sems.at[index],
            device_id=device, device_id_type=MESH,
        )

    def send(src, dst, index, device):
        copy = remote(src, dst, index, device)
        copy.start()
        pending.append(copy)

    def arrived(ref, index):
        remote(ref, ref, index, dev()).wait_recv()

    def rem(value, size):
        return lax.rem(value + size, size)

    sibling = dev(cc=1 - c)

    loads = [
        pltpu.make_async_copy(gate_hbm.at[0], wg, local_sems.at[0]),
        pltpu.make_async_copy(up_hbm.at[0], wu, local_sems.at[1]),
        pltpu.make_async_copy(down_hbm.at[0], wd, local_sems.at[2]),
    ]
    for load in loads:
        load.start()

    barrier = pltpu.get_barrier_semaphore()
    for j in range(1, groups):
        pl.semaphore_signal(barrier, inc=1, device_id=(rem(e + j, groups), t), device_id_type=MESH)
    for j in range(1, NX):
        pl.semaphore_signal(barrier, inc=1, device_id=dev(xx=rem(x + j, NX)), device_id_type=MESH)
    for j in range(1, nz):
        pl.semaphore_signal(barrier, inc=1, device_id=dev(zz=rem(z + j, nz)), device_id_type=MESH)

    def z_rows(block):
        return pl.ds(pl.multiple_of(x * slab + block * feat, feat), feat)

    stage_t[:, :feat] = tok_ref[...].astype(jnp.float32)
    stage_g[:, :feat] = grad_ref[...].astype(jnp.float32)
    xt[c, y, z_rows(z)] = stage_t[...].T[:feat].astype(jnp.bfloat16)
    gt[c, y, z_rows(z)] = stage_g[...].T[:feat].astype(jnp.bfloat16)
    for k in range(2):
        meta[e, k : k + 1] = cols_to_row(routes_ref, k, tokens)
        meta[e, 2 + k : 3 + k] = cols_to_row(values_ref, k, tokens)

    pl.semaphore_wait(barrier, groups - 1 + NX - 1 + nz - 1)

    right, left = dev(zz=rem(z + 1, nz)), dev(zz=rem(z - 1, nz))
    n_right, n_left = nz // 2, (nz - 1) // 2
    tr, gr = take(n_right), take(n_right)
    tl, gl = take(max(n_left, 1)), take(max(n_left, 1))

    def t_block(block):
        return xt.at[c, y, z_rows(block)]

    def g_block(block):
        return gt.at[c, y, z_rows(block)]

    for s in range(n_right):
        block = rem(z - s, nz)
        if s:
            arrived(t_block(block), tr + s - 1)
        send(t_block(block), t_block(block), tr + s, right)
        if s:
            arrived(g_block(block), gr + s - 1)
        send(g_block(block), g_block(block), gr + s, right)
        if s < n_left:
            block = rem(z + s, nz)
            if s:
                arrived(t_block(block), tl + s - 1)
            send(t_block(block), t_block(block), tl + s, left)
            if s:
                arrived(g_block(block), gl + s - 1)
            send(g_block(block), g_block(block), gl + s, left)
        if s == 0:
            meta_sems = take(groups)
            for j in range(1, groups):
                send(meta.at[e], meta.at[e], meta_sems + j, (rem(e + j, groups), t))
    arrived(t_block(rem(z - n_right, nz)), tr + n_right - 1)
    arrived(g_block(rem(z - n_right, nz)), gr + n_right - 1)
    if n_left:
        arrived(t_block(rem(z + n_left, nz)), tl + n_left - 1)
        arrived(g_block(rem(z + n_left, nz)), gl + n_left - 1)

    class Ring:
        def __init__(self, me, place, block):
            self.me, self.block = me, block
            self.right, self.left = place(rem(me + 1, 4)), place(rem(me - 1, 4))
            self.base = take(6)

        def region(self, offset, half):
            return self.block(rem(self.me + offset, 4), half)

        def start(self):
            for half, way, index in ((0, self.right, 0), (1, self.left, 2), (1, self.right, 1), (0, self.left, 3)):
                send(self.region(0, half), self.region(0, half), self.base + index, way)

        def forward(self):
            arrived(self.region(-1, 0), self.base + 0)
            send(self.region(-1, 0), self.region(-1, 0), self.base + 4, self.right)
            arrived(self.region(1, 1), self.base + 2)
            send(self.region(1, 1), self.region(1, 1), self.base + 5, self.left)

        def rest(self):
            return ((-1, 1, 1), (1, 0, 3), (2, 0, 4), (2, 1, 5))

        def wait(self, item):
            offset, half, index = item
            arrived(self.region(offset, half), self.base + index)

    def x_rows(block, half=None):
        if half is None:
            return pl.ds(pl.multiple_of(block * slab, slab), slab)
        return pl.ds(pl.multiple_of(block * slab + half * half_slab, half_slab), half_slab)

    def share(region):
        index = take()
        send(region, region, index, sibling)
        return index

    t_first = Ring(x, lambda p: dev(xx=p), lambda b, h: xt.at[c, y, x_rows(b, h)])
    g_first = Ring(y, lambda p: dev(yy=p), lambda b, h: gt.at[c, b, x_rows(x, h)])
    t_first.start()
    g_first.start()
    t_first.forward()
    g_first.forward()
    for item in t_first.rest():
        t_first.wait(item)
    half_depth = depth // 2
    t_last = Ring(y, lambda p: dev(yy=p), lambda b, h: xt.at[c, b, pl.ds(h * half_depth, half_depth)])
    t_last.start()
    for item in g_first.rest():
        g_first.wait(item)
    half_y = ny // 2
    g_last = Ring(x, lambda p: dev(xx=p), lambda b, h: gt.at[c, pl.ds(h * half_y, half_y), x_rows(b)])
    g_last.start()

    shared = []

    def share_t(offset, half):
        shared.append((lambda cc, o=offset, h=half: xt.at[cc, rem(y + o, 4), pl.ds(h * half_depth, half_depth)],
                       share(t_last.region(offset, half))))

    def share_g(offset, half):
        shared.append((lambda cc, o=offset, h=half: gt.at[cc, pl.ds(h * half_y, half_y), x_rows(rem(x + o, 4))],
                       share(g_last.region(offset, half))))

    for half in range(2):
        share_t(0, half)
        share_g(0, half)

    for load in loads:
        load.wait()
    ones = (
        lax.broadcasted_iota(jnp.int32, (hidden, hidden), 0)
        == lax.broadcasted_iota(jnp.int32, (hidden, hidden), 1)
    ).astype(jnp.bfloat16)

    @pl.loop(0, NX)
    def _(i):
        rows = pl.ds(pl.multiple_of(i * slab, slab), slab)
        for k, ref in enumerate((wg, wu)):
            wt[k * hidden : (k + 1) * hidden, rows] = lax.dot_general(
                ones, ref[rows, :], contract_cols, preferred_element_type=jnp.float32
            ).astype(jnp.bfloat16)

    t_last.forward()
    g_last.forward()
    share_t(-1, 0)
    share_t(1, 1)
    share_g(-1, 0)
    share_g(1, 1)
    for item in t_last.rest():
        t_last.wait(item)
        share_t(item[0], item[1])
    for item in g_last.rest():
        g_last.wait(item)
        share_g(item[0], item[1])
    for j in range(1, groups):
        arrived(meta.at[rem(e - j, groups)], meta_sems + j)
    for region, index in shared:
        arrived(region(1 - c), index)

    @pl.loop(0, ny)
    def _(p):
        rows = jnp.concatenate([xt[0, p], xt[1, p]], axis=1)
        grads = jnp.concatenate([gt[0, p], gt[1, p]], axis=1)
        pre = jnp.dot(wt[...], rows, preferred_element_type=jnp.float32)
        hidden_grad = jnp.dot(wd[...], grads, preferred_element_type=jnp.float32)
        pre_gate, pre_up = pre[:hidden], pre[hidden:]
        info = jnp.concatenate([meta[2 * p], meta[2 * p + 1]], axis=1)
        mine = e.astype(jnp.float32)
        hit0 = (info[0:1] == mine).astype(jnp.float32)
        hit1 = (info[1:2] == mine).astype(jnp.float32)
        weight = hit0 * info[2:3] + hit1 * info[3:4]
        s = jax.nn.sigmoid(pre_gate)
        activated = pre_gate * s
        slope = s * (1.0 + pre_gate * (1.0 - s))
        gate_partial = jnp.sum(activated * pre_up * hidden_grad, axis=0, keepdims=True)
        scaled = (weight * activated * pre_up).astype(jnp.bfloat16)
        gate_pre = (weight * hidden_grad * pre_up * slope).astype(jnp.bfloat16)
        up_pre = (weight * hidden_grad * activated).astype(jnp.bfloat16)
        for k in range(2):
            lanes = slice(k * tokens, (k + 1) * tokens)
            ab[k, p, :hidden] = gate_pre[:, lanes]
            ab[k, p, hidden:] = up_pre[:, lanes]
            hh[k, p] = scaled[:, lanes]
            vp[2 * p + k, 0:1] = (gate_partial * hit0)[:, lanes]
            vp[2 * p + k, 1:2] = (gate_partial * hit1)[:, lanes]

    v_sems = take(groups)
    for j in range(1, groups):
        peer = rem(e + j, groups)
        send(vp.at[peer], vr.at[e], v_sems + j, (peer, t))

    sib_sems = take(ny)
    a_sems = take(4)
    b_sems = take(16)

    def combine(j):
        yy = rem(y + 1 + j, ny)
        arrived(sib_in.at[yy], sib_sems + j)

        @pl.loop(0, NX)
        def _(i):
            s1[yy, i] = (own[yy, i] + sib_in[yy, i].astype(jnp.float32)).astype(jnp.bfloat16)

        if j < ny - 1:
            send(s1.at[yy, :, pl.ds(0, half_slab)], r1a.at[y], a_sems + j, dev(yy=yy))
        for k in range(1, NX):
            xx = rem(x + k, NX)
            send(s1.at[yy, xx, pl.ds(half_slab, half_slab)], r1b.at[x, yy], b_sems + 4 * j + k, dev(xx=xx))

    for j in range(ny):
        yy = rem(y + 1 + j, ny)

        @pl.loop(0, NX)
        def _(i):
            rows = pl.ds(pl.multiple_of(i * slab, slab), slab)
            weights = jnp.concatenate([wg[rows, :], wu[rows, :]], axis=1)
            pair = jnp.concatenate([ab[1 - c, yy], ab[c, yy]], axis=1)
            part = jnp.dot(weights, pair, preferred_element_type=jnp.float32)
            sib_out[yy, i] = part[:, :tokens].astype(jnp.bfloat16)
            own[yy, i] = part[:, tokens:]

        send(sib_out.at[yy], sib_in.at[yy], sib_sems + j, sibling)
        if j:
            combine(j - 1)
    combine(ny - 1)

    @pl.loop(0, NX)
    def _(i):
        rows = pl.ds(pl.multiple_of(i * slab, slab), slab)
        total = jnp.zeros((slab, 2 * hidden), jnp.float32)
        for p in range(ny):
            lhs = jnp.concatenate([xt[0, p, rows, :], xt[1, p, rows, :]], axis=1)
            rhs = jnp.concatenate([ab[0, p], ab[1, p]], axis=1)
            total += lax.dot_general(lhs, rhs, contract_cols, preferred_element_type=jnp.float32)
        og[rows, :] = total[:, :hidden].astype(jnp.bfloat16)
        ou[rows, :] = total[:, hidden:].astype(jnp.bfloat16)

    for j in range(1, groups):
        arrived(vr.at[rem(e - j, groups)], v_sems + j)
    vr[e] = vp[e]
    v1[...] = sum(vr[k] for k in range(groups))
    vx_sems = take(NX)
    for k in range(1, NX):
        send(v1, vx.at[x], vx_sems + k, dev(xx=rem(x + k, NX)))

    s2a_sems, s2b_sems = take(4), take(4)
    for j in range(ny - 1):
        src = rem(y - 1 - j, ny)
        arrived(r1a.at[src], a_sems + j)
    for j in range(NX):
        xx = rem(x + 1 + j, NX)
        total = own[y, xx, :half_slab] + sib_in[y, xx, :half_slab].astype(jnp.float32)
        for k in range(1, ny):
            total += r1a[rem(y - k, ny), xx].astype(jnp.float32)
        if j < NX - 1:
            s2a[xx] = total.astype(jnp.bfloat16)
            send(s2a.at[xx], r2a.at[x], s2a_sems + j, dev(xx=xx))
        else:
            s2fa[...] = total
    for j in range(ny):
        yy = rem(y + 1 + j, ny)
        for k in range(1, NX):
            arrived(r1b.at[rem(x - k, NX), yy], b_sems + 4 * j + k)
        total = own[yy, x, half_slab:] + sib_in[yy, x, half_slab:].astype(jnp.float32)
        for k in range(1, NX):
            total += r1b[rem(x - k, NX), yy].astype(jnp.float32)
        if j < ny - 1:
            s2b[yy] = total.astype(jnp.bfloat16)
            send(s2b.at[yy], r2b.at[y], s2b_sems + j, dev(yy=yy))
        else:
            s2fb[...] = total

    @pl.loop(0, NX)
    def _(i):
        rows = pl.ds(pl.multiple_of(i * slab, slab), slab)
        total = jnp.zeros((hidden, slab), jnp.float32)
        for p in range(ny):
            lhs = jnp.concatenate([hh[0, p], hh[1, p]], axis=1)
            rhs = jnp.concatenate([gt[0, p, rows, :], gt[1, p, rows, :]], axis=1)
            total += lax.dot_general(lhs, rhs, contract_cols, preferred_element_type=jnp.float32)
        od[:, rows] = total.astype(jnp.bfloat16)

    for k in range(1, NX):
        arrived(vx.at[rem(x - k, NX)], vx_sems + k)
    vx[x] = v1[...]
    vz[z] = sum(vx[k] for k in range(NX))
    vz_sems = take(nz)
    for k in range(1, nz):
        send(vz.at[z], vz.at[z], vz_sems + k, dev(zz=rem(z + k, nz)))

    for j in range(NX - 1):
        arrived(r2a.at[rem(x - 1 - j, NX)], s2a_sems + j)
        arrived(r2b.at[rem(y - 1 - j, ny)], s2b_sems + j)
    total = s2fa[...]
    for k in range(1, NX):
        total += r2a[rem(x - k, NX)].astype(jnp.float32)
    s3f[:half_slab] = total
    s3[:half_slab] = total.astype(jnp.bfloat16)
    total = s2fb[...]
    for k in range(1, ny):
        total += r2b[rem(y - k, ny)].astype(jnp.float32)
    s3f[half_slab:] = total
    s3[half_slab:] = total.astype(jnp.bfloat16)

    s3_sems = take(nz)
    for k in range(1, nz):
        zz = rem(z + k, nz)
        rows = pl.ds(pl.multiple_of(zz * feat, feat), feat)
        send(s3.at[rows], r3.at[z], s3_sems + k, dev(zz=zz))

    stores = [
        pltpu.make_async_copy(og, ggrad_hbm.at[0], local_sems.at[3]),
        pltpu.make_async_copy(ou, ugrad_hbm.at[0], local_sems.at[4]),
        pltpu.make_async_copy(od, dgrad_hbm.at[0], local_sems.at[5]),
    ]
    for store in stores:
        store.start()

    for k in range(1, nz):
        arrived(vz.at[rem(z - k, nz)], vz_sems + k)
    sums = sum(vz[k] for k in range(nz))
    lane = lax.broadcasted_iota(jnp.int32, (tokens, 2), 1)
    vgrad_ref[...] = jnp.where(
        lane == 0, row_to_col(sums[0:1], tokens), row_to_col(sums[1:2], tokens)
    )

    for k in range(1, nz):
        arrived(r3.at[rem(z - k, nz)], s3_sems + k)
    result = s3f[pl.ds(pl.multiple_of(z * feat, feat), feat)]
    for k in range(1, nz):
        result += r3[rem(z - k, nz)].astype(jnp.float32)
    stage_t[:feat] = result
    tgrad_ref[...] = stage_t[...].T[:, :feat].astype(jnp.bfloat16)

    for store in stores:
        store.wait()
    for copy in pending:
        copy.wait_send()
    assert counter[0] <= send_sems.shape[0], counter[0]


def per_device(tokens, out_grad, routes, gate_values, gate_weight, up_weight, down_weight):
    groups = lax.axis_size("expert")
    ny, nz = groups // 2, lax.axis_size("tensor") // NX
    count, feat = tokens.shape
    depth, hidden = gate_weight.shape[1:]
    slab, half_slab = nz * feat, nz * feat // 2
    f32, bf16 = jnp.float32, jnp.bfloat16
    vmem = pl.BlockSpec(memory_space=pltpu.VMEM)
    hbm = pl.BlockSpec(memory_space=pl.ANY)
    scratch = [
        ((2, ny, depth, count), bf16),
        ((2, ny, depth, count), bf16),
        ((groups, 8, count), f32),
        ((depth, hidden), bf16),
        ((depth, hidden), bf16),
        ((hidden, depth), bf16),
        ((2 * hidden, depth), bf16),
        ((2, ny, 2 * hidden, count), bf16),
        ((2, ny, hidden, count), bf16),
        ((ny, NX, slab, count), f32),
        ((ny, NX, slab, count), bf16),
        ((ny, NX, slab, count), bf16),
        ((ny, NX, slab, count), bf16),
        ((ny, NX, half_slab, count), bf16),
        ((NX, ny, half_slab, count), bf16),
        ((NX, half_slab, count), bf16),
        ((ny, half_slab, count), bf16),
        ((half_slab, count), f32),
        ((half_slab, count), f32),
        ((NX, half_slab, count), bf16),
        ((ny, half_slab, count), bf16),
        ((slab, count), bf16),
        ((slab, count), f32),
        ((nz, feat, count), bf16),
        ((groups, 8, count), f32),
        ((groups, 8, count), f32),
        ((8, count), f32),
        ((NX, 8, count), f32),
        ((nz, 8, count), f32),
        ((depth, hidden), bf16),
        ((depth, hidden), bf16),
        ((hidden, depth), bf16),
        ((count, 128), f32),
        ((count, 128), f32),
    ]
    flops = 2 * groups * count * depth * hidden * 8
    return pl.pallas_call(
        functools.partial(kernel, (ny, nz, feat, count, hidden)),
        out_shape=(
            jax.ShapeDtypeStruct(tokens.shape, bf16),
            jax.ShapeDtypeStruct(gate_values.shape, f32),
            jax.ShapeDtypeStruct(gate_weight.shape, bf16),
            jax.ShapeDtypeStruct(up_weight.shape, bf16),
            jax.ShapeDtypeStruct(down_weight.shape, bf16),
        ),
        in_specs=[vmem] * 4 + [hbm] * 3,
        out_specs=(vmem, vmem, hbm, hbm, hbm),
        scratch_shapes=[pltpu.VMEM(shape, dtype) for shape, dtype in scratch]
        + [
            pltpu.SemaphoreType.DMA((200,)),
            pltpu.SemaphoreType.DMA((200,)),
            pltpu.SemaphoreType.DMA((6,)),
        ],
        compiler_params=pltpu.CompilerParams(
            collective_id=0, has_side_effects=True, vmem_limit_bytes=48 * 1024 * 1024
        ),
        cost_estimate=pl.CostEstimate(
            flops=flops, bytes_accessed=2**22, transcendentals=groups * count * hidden
        ),
    )(tokens, out_grad, routes, gate_values, gate_weight, up_weight, down_weight)


def solution(mesh):
    in_specs = (
        P("expert", "tensor"),
        P("expert", "tensor"),
        P("expert", None),
        P("expert", None),
        P("expert", None, "tensor"),
        P("expert", None, "tensor"),
        P("expert", "tensor", None),
    )
    out_specs = (
        P("expert", "tensor"),
        P("expert", None),
        P("expert", None, "tensor"),
        P("expert", None, "tensor"),
        P("expert", "tensor", None),
    )
    return jax.shard_map(
        per_device, mesh=mesh, in_specs=in_specs, out_specs=out_specs, check_vma=False
    )
```

```python
import functools

import jax
import jax.numpy as jnp
from jax import lax
from jax.experimental import pallas as pl
from jax.experimental.pallas import tpu as pltpu
from jax.sharding import PartitionSpec as P

MESH = pl.DeviceIdType.MESH
NX = 4
DIRECT = (0, 3)
SLOT = {1: 0, 3: 1, 2: 2}
contract_cols = (((1,), (1,)), ((), ()))


def kernel(
    dims,
    tok_ref, grad_ref, routes_ref, values_ref, gate_hbm, up_hbm, down_hbm,
    tgrad_ref, vgrad_ref, ggrad_hbm, ugrad_hbm, dgrad_hbm,
    xg, meta, wg, wu, wd, wt, pre, hg, ab, hh, own, sib_out, sib_in, s1, r1a, r1b,
    s2a, s2b, s2fa, s2fb, r2a, r2b, s3, s3f, r3, vp, vr, v1, vx, vz,
    og, ou, od, send_sems, recv_sems, local_sems,
):
    ny, nz, nq, feat, tokens, hidden = dims
    e = lax.axis_index("expert")
    t = lax.axis_index("tensor")
    y, c = e // 2, e % 2
    x, z = t // nz, t % nz
    qz = nz // nq
    k, i = z // qz, z % qz
    slab = nz * feat
    quad = qz * feat
    half = quad // 2
    groups = 2 * ny
    quad_order = [0, 1, 3, 2][:nq] if nq == 4 else [0, 1]
    f32, bf16 = jnp.float32, jnp.bfloat16

    counter = [0]
    pending = []

    def rem(value, size):
        return lax.rem(value + size, size)

    def dev(xx=None, yy=None, zz=None, cc=None):
        xx = x if xx is None else xx
        yy = y if yy is None else yy
        zz = z if zz is None else zz
        cc = c if cc is None else cc
        return (yy * 2 + cc, xx * nz + zz)

    def take(count=1):
        first = counter[0]
        counter[0] += count
        return first

    def remote(src, dst, index, device):
        return pltpu.make_async_remote_copy(
            src_ref=src, dst_ref=dst, send_sem=send_sems.at[index], recv_sem=recv_sems.at[index],
            device_id=device, device_id_type=MESH,
        )

    def send(src, dst, index, device):
        copy = remote(src, dst, index, device)
        copy.start()
        pending.append(copy)

    def arrived(ref, index):
        remote(ref, ref, index, dev()).wait_recv()

    sibling = dev(cc=1 - c)

    def drain():
        for copy in pending:
            copy.wait_send()
        pending.clear()

    loads = [
        pltpu.make_async_copy(gate_hbm.at[0], wg, local_sems.at[0]),
        pltpu.make_async_copy(up_hbm.at[0], wu, local_sems.at[1]),
        pltpu.make_async_copy(down_hbm.at[0], wd, local_sems.at[2]),
    ]
    for load in loads:
        load.start()

    barrier = pltpu.get_barrier_semaphore()
    for j in range(1, groups):
        pl.semaphore_signal(barrier, inc=1, device_id=(rem(e + j, groups), t), device_id_type=MESH)
    for j in range(1, NX):
        pl.semaphore_signal(barrier, inc=1, device_id=dev(xx=rem(x + j, NX)), device_id_type=MESH)
    for j in range(1, nz):
        pl.semaphore_signal(barrier, inc=1, device_id=dev(zz=rem(z + j, nz)), device_id_type=MESH)

    def feats(block):
        return pl.ds(pl.multiple_of(block * feat, feat), feat)

    xg[0, c, y, x, feats(z)] = tok_ref[...]
    xg[1, c, y, x, feats(z)] = grad_ref[...]
    meta[e, 0:2] = routes_ref[...].astype(f32)
    meta[e, 2:4] = values_ref[...].astype(f32)
    pl.semaphore_wait(barrier, groups - 1 + NX - 1 + nz - 1)

    def z_block(block):
        return xg.at[:, c, y, x, feats(block)]

    z_sems = take(nz)

    def z_start(u):
        for s in range(1 if u == 0 else 0, qz):
            zz = rem(k + quad_order[u], nq) * qz + rem(i + s, qz)
            send(z_block(z), z_block(z), z_sems + u * qz + s, dev(zz=zz))

    z_start(0)
    meta_sems = take(groups)
    for j in range(1, groups):
        send(meta.at[e], meta.at[e], meta_sems + j, (rem(e + j, groups), t))

    for load in loads:
        load.wait()
    ones = (
        lax.broadcasted_iota(jnp.int32, (hidden, hidden), 0)
        == lax.broadcasted_iota(jnp.int32, (hidden, hidden), 1)
    ).astype(bf16)

    @pl.loop(0, NX)
    def _(n):
        rows = pl.ds(pl.multiple_of(n * slab, slab), slab)
        for m, ref in enumerate((wg, wu)):
            wt[m * hidden : (m + 1) * hidden, rows] = lax.dot_general(
                ones, ref[rows, :], contract_cols, preferred_element_type=f32
            ).astype(bf16)

    def source_quad(u):
        return rem(k - quad_order[u], nq)

    def rows_of(q):
        return pl.ds(pl.multiple_of(q * quad, quad), quad)

    first_sems = [take(6) for _ in range(nq)]
    last_sems = [take(8) for _ in range(nq)]
    share_sems = [take(10) for _ in range(nq)]
    shared = [[] for _ in range(nq)]

    def first_start(u):
        q = source_quad(u)
        for s in range(1 if u == 0 else 0, qz):
            arrived(z_block(q * qz + rem(i - s, qz)), z_sems + u * qz + s)
        for j in (1, 3, 2):
            mine = xg.at[0, c, y, x, rows_of(q)]
            send(mine, mine, first_sems[u] + j - 1, dev(xx=rem(x + j, NX)))
            mine = xg.at[1, c, y, x, rows_of(q)]
            send(mine, mine, first_sems[u] + 3 + j - 1, dev(yy=rem(y + j, ny)))

    def t_part(cc, offset, q, part=None):
        cols = pl.ds(0, NX) if part is None else pl.ds(part * (NX // 2), NX // 2)
        return xg.at[0, cc, rem(y + offset + ny, ny), cols, rows_of(q)]

    def g_part(cc, offset, q, part=None):
        cols = pl.ds(0, ny) if part is None else pl.ds(part * (ny // 2), ny // 2)
        return xg.at[1, cc, cols, rem(x + offset + NX, NX), rows_of(q)]

    def share(u, region, offset, part=None):
        q = source_quad(u)
        index = share_sems[u] + len(shared[u])
        send(region(c, offset, q, part), region(c, offset, q, part), index, sibling)
        shared[u].append((region(1 - c, offset, q, part), index))

    def last_start(u):
        q = source_quad(u)
        for j in (1, 3, 2):
            arrived(xg.at[0, c, y, rem(x - j, NX), rows_of(q)], first_sems[u] + j - 1)
        ways = (1, 3, 2) if u in DIRECT else (1, 3)
        for j in ways:
            mine = t_part(c, 0, q)
            send(mine, mine, last_sems[u] + SLOT[j], dev(yy=rem(y + j, ny)))
        for j in (1, 3, 2):
            arrived(xg.at[1, c, rem(y - j, ny), x, rows_of(q)], first_sems[u] + 3 + j - 1)
        for j in ways:
            mine = g_part(c, 0, q)
            send(mine, mine, last_sems[u] + 4 + SLOT[j], dev(xx=rem(x + j, NX)))
        share(u, t_part, 0)
        share(u, g_part, 0)

    def last_forward(u):
        if u in DIRECT:
            return
        q = source_quad(u)
        for way in (0, 1):
            step = 1 - 2 * way
            arrived(t_part(c, -step, q), last_sems[u] + way)
            part = t_part(c, -step, q, way)
            send(part, part, last_sems[u] + 2 + way, dev(yy=rem(y + step, ny)))
            arrived(g_part(c, -step, q), last_sems[u] + 4 + way)
            part = g_part(c, -step, q, way)
            send(part, part, last_sems[u] + 6 + way, dev(xx=rem(x + step, NX)))
        for step in (1, -1):
            share(u, t_part, -step)
            share(u, g_part, -step)

    def last_finish(u):
        q = source_quad(u)
        if u in DIRECT:
            for j in (1, 3, 2):
                arrived(t_part(c, -j, q), last_sems[u] + SLOT[j])
                share(u, t_part, -j)
                arrived(g_part(c, -j, q), last_sems[u] + 4 + SLOT[j])
                share(u, g_part, -j)
            return
        for way in (0, 1):
            arrived(t_part(c, 2, q, way), last_sems[u] + 2 + way)
            share(u, t_part, 2, way)
            arrived(g_part(c, 2, q, way), last_sems[u] + 6 + way)
            share(u, g_part, 2, way)

    def product(u):
        q = source_quad(u)
        for region, index in shared[u]:
            arrived(region, index)
        spans = [
            pl.ds(pl.multiple_of(n * slab + q * quad, quad), quad) for n in range(NX)
        ]

        @pl.loop(0, ny)
        def _(p):
            lhs = jnp.concatenate([wt[:, span] for span in spans], axis=1)
            rhs = jnp.concatenate(
                [
                    jnp.concatenate([xg[0, 0, p, n, rows_of(q)], xg[0, 1, p, n, rows_of(q)]], axis=1)
                    for n in range(NX)
                ],
                axis=0,
            )
            part = jnp.dot(lhs, rhs, preferred_element_type=f32)
            pre[p] = part if u == 0 else pre[p] + part
            lhs = jnp.concatenate([wd[:, span] for span in spans], axis=1)
            rhs = jnp.concatenate(
                [
                    jnp.concatenate([xg[1, 0, p, n, rows_of(q)], xg[1, 1, p, n, rows_of(q)]], axis=1)
                    for n in range(NX)
                ],
                axis=0,
            )
            part = jnp.dot(lhs, rhs, preferred_element_type=f32)
            hg[p] = part if u == 0 else hg[p] + part

    if nq == 4:
        first_start(0)
        z_start(1)
        z_start(2)
        last_start(0)
        z_start(3)
        last_forward(0)
        first_start(1)
        first_start(2)
        last_finish(0)
        last_start(1)
        last_start(2)
        first_start(3)
        product(0)
        last_forward(1)
        last_forward(2)
        last_start(3)
        last_finish(1)
        last_finish(2)
        product(1)
        product(2)
        last_forward(3)
        last_finish(3)
        product(3)
    else:
        for u in range(nq):
            if u:
                z_start(u)
            first_start(u)
            last_start(u)
            last_forward(u)
            last_finish(u)
            product(u)
    for j in range(1, groups):
        arrived(meta.at[rem(e - j, groups)], meta_sems + j)

    @pl.loop(0, ny)
    def _(p):
        pre_gate, pre_up, hidden_grad = pre[p, :hidden], pre[p, hidden:], hg[p]
        info = jnp.concatenate([meta[2 * p], meta[2 * p + 1]], axis=1)
        mine = e.astype(f32)
        hit0 = (info[0:1] == mine).astype(f32)
        hit1 = (info[1:2] == mine).astype(f32)
        weight = hit0 * info[2:3] + hit1 * info[3:4]
        s = jax.nn.sigmoid(pre_gate)
        activated = pre_gate * s
        slope = s * (1.0 + pre_gate * (1.0 - s))
        gate_partial = jnp.sum(activated * pre_up * hidden_grad, axis=0, keepdims=True)
        scaled = (weight * activated * pre_up).astype(bf16)
        gate_pre = (weight * hidden_grad * pre_up * slope).astype(bf16)
        up_pre = (weight * hidden_grad * activated).astype(bf16)
        for m in range(2):
            lanes = slice(m * tokens, (m + 1) * tokens)
            ab[m, p, :hidden] = gate_pre[:, lanes]
            ab[m, p, hidden:] = up_pre[:, lanes]
            hh[m, p] = scaled[:, lanes]
            vp[2 * p + m, 0:1] = (gate_partial * hit0)[:, lanes]
            vp[2 * p + m, 1:2] = (gate_partial * hit1)[:, lanes]

    sum_order = quad_order[::-1]
    sib_sems = take(nq)
    s1_sems = [take(6) for _ in range(nq)]
    s2_sems = [take(6) for _ in range(nq)]
    s3_sems = take(nz)

    def target_quad(u):
        return rem(k + sum_order[u], nq)

    def input_grads(u):
        q = target_quad(u)

        @pl.loop(0, ny)
        def _(p):
            spans = [
                pl.ds(pl.multiple_of(n * slab + q * quad, quad), quad) for n in range(NX)
            ]
            weights = jnp.concatenate(
                [jnp.concatenate([wg[span, :], wu[span, :]], axis=1) for span in spans], axis=0
            )
            pair = jnp.concatenate([ab[1 - c, p], ab[c, p]], axis=1)
            part = jnp.dot(weights, pair, preferred_element_type=f32)
            for n in range(NX):
                sib_out[q, p, n] = part[n * quad : (n + 1) * quad, :tokens].astype(bf16)
                own[q, p, n] = part[n * quad : (n + 1) * quad, tokens:]

        send(sib_out.at[q], sib_in.at[q], sib_sems + u, sibling)

    def first_sum(u):
        q = target_quad(u)
        arrived(sib_in.at[q], sib_sems + u)

        @pl.loop(0, ny)
        def _(p):
            s1[q, p] = (own[q, p] + sib_in[q, p].astype(f32)).astype(bf16)

        for j in (2, 1, 3):
            yy, xx = rem(y + j, ny), rem(x + j, NX)
            send(s1.at[q, yy, :, pl.ds(0, half)], r1a.at[q, y], s1_sems[u] + j - 1, dev(yy=yy))
            send(s1.at[q, :, xx, pl.ds(half, half)], r1b.at[q, x], s1_sems[u] + 3 + j - 1, dev(xx=xx))

    def second_sum(u):
        q = target_quad(u)
        for j in (1, 2, 3):
            arrived(r1a.at[q, rem(y - j, ny)], s1_sems[u] + j - 1)
        for j in (2, 1, 3, 0):
            xx = rem(x + j, NX)
            total = own[q, y, xx, :half] + sib_in[q, y, xx, :half].astype(f32)
            for m in range(1, ny):
                total += r1a[q, rem(y - m, ny), xx].astype(f32)
            if j:
                s2a[q, xx] = total.astype(bf16)
                send(s2a.at[q, xx], r2a.at[q, x], s2_sems[u] + j - 1, dev(xx=xx))
            else:
                s2fa[q] = total
        for j in (1, 2, 3):
            arrived(r1b.at[q, rem(x - j, NX)], s1_sems[u] + 3 + j - 1)
        for j in (2, 1, 3, 0):
            yy = rem(y + j, ny)
            total = own[q, yy, x, half:] + sib_in[q, yy, x, half:].astype(f32)
            for m in range(1, NX):
                total += r1b[q, rem(x - m, NX), yy].astype(f32)
            if j:
                s2b[q, yy] = total.astype(bf16)
                send(s2b.at[q, yy], r2b.at[q, y], s2_sems[u] + 3 + j - 1, dev(yy=yy))
            else:
                s2fb[q] = total

    def third_sum(u):
        q = target_quad(u)
        for j in (1, 2, 3):
            arrived(r2a.at[q, rem(x - j, NX)], s2_sems[u] + j - 1)
        total = s2fa[q]
        for m in range(1, NX):
            total += r2a[q, rem(x - m, NX)].astype(f32)
        s3f[q, :half] = total
        s3[q, :half] = total.astype(bf16)
        for j in (1, 2, 3):
            arrived(r2b.at[q, rem(y - j, ny)], s2_sems[u] + 3 + j - 1)
        total = s2fb[q]
        for m in range(1, ny):
            total += r2b[q, rem(y - m, ny)].astype(f32)
        s3f[q, half:] = total
        s3[q, half:] = total.astype(bf16)
        for s in range(1 if sum_order[u] == 0 else 0, qz):
            place = rem(i + s, qz)
            slot = u * qz + s
            send(s3.at[q, feats(place)], r3.at[slot], s3_sems + slot, dev(zz=q * qz + place))

    def gate_up_grads(n):
        rows = slice(n * slab, (n + 1) * slab)
        total = jnp.zeros((slab, 2 * hidden), f32)
        for p in range(ny):
            lhs = jnp.concatenate([xg[0, 0, p, n], xg[0, 1, p, n]], axis=1)
            rhs = jnp.concatenate([ab[0, p], ab[1, p]], axis=1)
            total += lax.dot_general(lhs, rhs, contract_cols, preferred_element_type=f32)
        og[rows, :] = total[:, :hidden].astype(bf16)
        ou[rows, :] = total[:, hidden:].astype(bf16)

    def down_grads(n):
        total = jnp.zeros((hidden, slab), f32)
        for p in range(ny):
            lhs = jnp.concatenate([hh[0, p], hh[1, p]], axis=1)
            rhs = jnp.concatenate([xg[1, 0, p, n], xg[1, 1, p, n]], axis=1)
            total += lax.dot_general(lhs, rhs, contract_cols, preferred_element_type=f32)
        od[:, n * slab : (n + 1) * slab] = total.astype(bf16)

    v_sems, vx_sems, vz_sems = take(groups), take(NX), take(nz)

    def values_start():
        for j in range(1, groups):
            peer = rem(e + j, groups)
            send(vp.at[peer], vr.at[e], v_sems + j, (peer, t))

    def values_x():
        for j in range(1, groups):
            arrived(vr.at[rem(e - j, groups)], v_sems + j)
        vr[e] = vp[e]
        v1[...] = sum(vr[m] for m in range(groups))
        for m in range(1, NX):
            send(v1, vx.at[x], vx_sems + m, dev(xx=rem(x + m, NX)))

    def values_z():
        for m in range(1, NX):
            arrived(vx.at[rem(x - m, NX)], vx_sems + m)
        vx[x] = v1[...]
        vz[z] = sum(vx[m] for m in range(NX))
        for m in range(1, nz):
            send(vz.at[z], vz.at[z], vz_sems + m, dev(zz=rem(z + m, nz)))

    stores = [
        pltpu.make_async_copy(og, ggrad_hbm.at[0], local_sems.at[3]),
        pltpu.make_async_copy(ou, ugrad_hbm.at[0], local_sems.at[4]),
        pltpu.make_async_copy(od, dgrad_hbm.at[0], local_sems.at[5]),
    ]

    for u in range(nq):
        input_grads(u)
    values_start()
    for u in range(nq):
        first_sum(u)
    values_x()
    drain()
    gate_up_grads(0)
    gate_up_grads(1)
    second_sum(0)
    gate_up_grads(2)
    gate_up_grads(3)
    stores[0].start()
    stores[1].start()
    second_sum(1)
    third_sum(0)
    values_z()
    down_grads(0)
    down_grads(1)
    for u in range(2, nq):
        second_sum(u)
        third_sum(u - 1)
        if u == 2:
            down_grads(2)
            down_grads(3)
            stores[2].start()
    if nq == 2:
        down_grads(2)
        down_grads(3)
        stores[2].start()
    third_sum(nq - 1)

    for m in range(1, nz):
        arrived(vz.at[rem(z - m, nz)], vz_sems + m)
    vgrad_ref[...] = sum(vz[m] for m in range(nz))[0:2]

    result = s3f[k, feats(i)]
    for u in range(nq):
        for s in range(1 if sum_order[u] == 0 else 0, qz):
            slot = u * qz + s
            arrived(r3.at[slot], s3_sems + slot)
            result += r3[slot].astype(f32)
    tgrad_ref[...] = result.astype(bf16)

    for store in stores:
        store.wait()

    drain()
    assert counter[0] <= send_sems.shape[0], counter[0]


def copies(count, *refs):
    sources, targets, held = refs[:count], refs[count : 2 * count], refs[2 * count : 3 * count]
    in_sems, out_sems = refs[3 * count :]
    ins = [pltpu.make_async_copy(sources[n], held[n], in_sems.at[n]) for n in range(count)]
    outs = [pltpu.make_async_copy(held[n], targets[n], out_sems.at[n]) for n in range(count)]
    for move in ins:
        move.start()
    for n in range(count):
        ins[n].wait()
        outs[n].start()
    for move in outs:
        move.wait()


def per_device(tokens, out_grad, routes, gate_values, gate_weight, up_weight, down_weight):
    groups = lax.axis_size("expert")
    ny, nz = groups // 2, lax.axis_size("tensor") // NX
    nq = 4 if nz >= 16 else 2
    count, feat = tokens.shape
    depth, hidden = gate_weight.shape[1:]
    slab, quad = nz * feat, nz // nq * feat
    half = quad // 2
    f32, bf16 = jnp.float32, jnp.bfloat16
    vmem = pl.BlockSpec(memory_space=pltpu.VMEM)
    hbm = pl.BlockSpec(memory_space=pl.ANY)
    scratch = [
        ((2, 2, ny, NX, slab, count), bf16),
        ((groups, 8, count), f32),
        ((depth, hidden), bf16),
        ((depth, hidden), bf16),
        ((hidden, depth), bf16),
        ((2 * hidden, depth), bf16),
        ((ny, 2 * hidden, 2 * count), f32),
        ((ny, hidden, 2 * count), f32),
        ((2, ny, 2 * hidden, count), bf16),
        ((2, ny, hidden, count), bf16),
        ((nq, ny, NX, quad, count), f32),
        ((nq, ny, NX, quad, count), bf16),
        ((nq, ny, NX, quad, count), bf16),
        ((nq, ny, NX, quad, count), bf16),
        ((nq, ny, NX, half, count), bf16),
        ((nq, NX, ny, half, count), bf16),
        ((nq, NX, half, count), bf16),
        ((nq, ny, half, count), bf16),
        ((nq, half, count), f32),
        ((nq, half, count), f32),
        ((nq, NX, half, count), bf16),
        ((nq, ny, half, count), bf16),
        ((nq, quad, count), bf16),
        ((nq, quad, count), f32),
        ((nz, feat, count), bf16),
        ((groups, 8, count), f32),
        ((groups, 8, count), f32),
        ((8, count), f32),
        ((NX, 8, count), f32),
        ((nz, 8, count), f32),
        ((depth, hidden), bf16),
        ((depth, hidden), bf16),
        ((hidden, depth), bf16),
    ]
    flops = 2 * groups * count * depth * hidden * 8
    out_shape = (
        jax.ShapeDtypeStruct((feat, count), bf16),
        jax.ShapeDtypeStruct((2, count), f32),
        jax.ShapeDtypeStruct(gate_weight.shape, bf16),
        jax.ShapeDtypeStruct(up_weight.shape, bf16),
        jax.ShapeDtypeStruct(down_weight.shape, bf16),
    )
    results = pl.pallas_call(
        functools.partial(kernel, (ny, nz, nq, feat, count, hidden)),
        out_shape=out_shape,
        in_specs=[vmem] * 4 + [hbm] * 3,
        out_specs=(vmem, vmem, hbm, hbm, hbm),
        scratch_shapes=[pltpu.VMEM(shape, dtype) for shape, dtype in scratch]
        + [
            pltpu.SemaphoreType.DMA((280,)),
            pltpu.SemaphoreType.DMA((280,)),
            pltpu.SemaphoreType.DMA((6,)),
        ],
        compiler_params=pltpu.CompilerParams(
            collective_id=0, has_side_effects=True, vmem_limit_bytes=60 * 1024 * 1024
        ),
        cost_estimate=pl.CostEstimate(
            flops=flops, bytes_accessed=2**22, transcendentals=groups * count * hidden
        ),
    )(tokens.T, out_grad.T, routes.T, gate_values.T, gate_weight, up_weight, down_weight)
    tokens_grad, values_grad, *weight_grads = pl.pallas_call(
        functools.partial(copies, len(results)),
        out_shape=out_shape,
        in_specs=[hbm] * len(results),
        out_specs=[hbm] * len(results),
        scratch_shapes=[pltpu.VMEM(result.shape, result.dtype) for result in results]
        + [pltpu.SemaphoreType.DMA((len(results),))] * 2,
        compiler_params=pltpu.CompilerParams(vmem_limit_bytes=60 * 1024 * 1024),
    )(*results)
    return (tokens_grad.T, values_grad.T, *weight_grads)


def solution(mesh):
    in_specs = (
        P("expert", "tensor"),
        P("expert", "tensor"),
        P("expert", None),
        P("expert", None),
        P("expert", None, "tensor"),
        P("expert", None, "tensor"),
        P("expert", "tensor", None),
    )
    out_specs = (
        P("expert", "tensor"),
        P("expert", None),
        P("expert", None, "tensor"),
        P("expert", None, "tensor"),
        P("expert", "tensor", None),
    )
    return jax.shard_map(
        per_device, mesh=mesh, in_specs=in_specs, out_specs=out_specs, check_vma=False
    )
```

```python
import functools

import jax
import jax.numpy as jnp
from jax import lax
from jax.experimental import pallas as pl
from jax.experimental.pallas import tpu as pltpu
from jax.sharding import PartitionSpec as P

MESH = pl.DeviceIdType.MESH
NX = 4
DIRECT = (0, 3)
SLOT = {1: 0, 3: 1, 2: 2}
contract_cols = (((1,), (1,)), ((), ()))


def kernel(
    dims,
    tok_ref, grad_ref, routes_ref, values_ref, gate_hbm, up_hbm, down_hbm,
    tgrad_ref, vgrad_ref, ggrad_hbm, ugrad_hbm, dgrad_hbm,
    xg, meta, wg, wu, wd, wt, pre, hg, ab, hh, own, s1, r1a, r1b,
    s2a, s2b, s2fa, s2fb, r2a, r2b, s3, s3f, r3, vp, vr, v1, vx, vz,
    og, ou, od, gu_own, gu_out, gu_in, d_own, d_out, d_in, rt, vl, send_sems, recv_sems, local_sems,
):
    ny, nz, nq, feat, tokens, hidden = dims
    e = lax.axis_index("expert")
    t = lax.axis_index("tensor")
    y, c = e // 2, e % 2
    x, z = t // nz, t % nz
    qz = nz // nq
    k, i = z // qz, z % qz
    slab = nz * feat
    quad = qz * feat
    half = quad // 2
    groups = 2 * ny
    quad_order = [0, 1, 3, 2][:nq] if nq == 4 else [0, 1]
    f32, bf16 = jnp.float32, jnp.bfloat16

    counter = [0]
    pending = []

    def rem(value, size):
        return lax.rem(value + size, size)

    def dev(xx=None, yy=None, zz=None, cc=None):
        xx = x if xx is None else xx
        yy = y if yy is None else yy
        zz = z if zz is None else zz
        cc = c if cc is None else cc
        return (yy * 2 + cc, xx * nz + zz)

    def take(count=1):
        first = counter[0]
        counter[0] += count
        return first

    def remote(src, dst, index, device):
        return pltpu.make_async_remote_copy(
            src_ref=src, dst_ref=dst, send_sem=send_sems.at[index], recv_sem=recv_sems.at[index],
            device_id=device, device_id_type=MESH,
        )

    def send(src, dst, index, device):
        copy = remote(src, dst, index, device)
        copy.start()
        pending.append(copy)

    def arrived(ref, index):
        remote(ref, ref, index, dev()).wait_recv()

    sibling = dev(cc=1 - c)

    def drain():
        for copy in pending:
            copy.wait_send()
        pending.clear()

    def feats(block):
        return pl.ds(pl.multiple_of(block * feat, feat), feat)

    inputs = [
        pltpu.make_async_copy(tok_ref, xg.at[0, y, x, feats(z)], local_sems.at[6]),
        pltpu.make_async_copy(grad_ref, xg.at[1, y, x, feats(z)], local_sems.at[7]),
        pltpu.make_async_copy(routes_ref, rt, local_sems.at[8]),
        pltpu.make_async_copy(values_ref, vl, local_sems.at[9]),
    ]
    for load in inputs:
        load.start()

    loads = [
        pltpu.make_async_copy(gate_hbm.at[0], wg.at[c], local_sems.at[0]),
        pltpu.make_async_copy(up_hbm.at[0], wu.at[c], local_sems.at[1]),
        pltpu.make_async_copy(down_hbm.at[0], wd.at[c], local_sems.at[2]),
    ]
    for load in loads:
        load.start()

    barrier = pltpu.get_barrier_semaphore()
    for j in range(nz // 2, 0, -1):
        for zz in sorted({j, nz - j}):
            pl.semaphore_signal(barrier, inc=1, device_id=dev(zz=rem(z + zz, nz)), device_id_type=MESH)
    for j in range(1, NX):
        pl.semaphore_signal(barrier, inc=1, device_id=dev(xx=rem(x + j, NX)), device_id_type=MESH)
    for j in range(1, ny):
        pl.semaphore_signal(barrier, inc=1, device_id=dev(yy=rem(y + j, ny)), device_id_type=MESH)
    pl.semaphore_signal(barrier, inc=1, device_id=sibling, device_id_type=MESH)

    for load in inputs:
        load.wait()
    meta[y, 0:2] = rt[...].astype(f32)
    meta[y, 2:4] = vl[...].astype(f32)
    pl.semaphore_wait(barrier, ny - 1 + NX - 1 + nz - 1 + 1)

    def z_block(block):
        return xg.at[:, y, x, feats(block)]

    z_sems = take(nz)

    def z_start(u):
        for s in range(1 if u == 0 else 0, qz):
            zz = rem(k + quad_order[u], nq) * qz + rem(i + s, qz)
            send(z_block(z), z_block(z), z_sems + u * qz + s, dev(zz=zz))

    z_start(0)
    meta_sems = take(ny)
    for j in range(1, ny):
        send(meta.at[y], meta.at[y], meta_sems + j, dev(yy=rem(y + j, ny)))

    for load in loads:
        load.wait()
    w_sems = take(3)
    for n, ref in enumerate((wg, wu, wd)):
        send(ref.at[c], ref.at[c], w_sems + n, sibling)
    ones = (
        lax.broadcasted_iota(jnp.int32, (hidden, hidden), 0)
        == lax.broadcasted_iota(jnp.int32, (hidden, hidden), 1)
    ).astype(bf16)

    def transpose(core):
        @pl.loop(0, NX)
        def _(n):
            rows = pl.ds(pl.multiple_of(n * slab, slab), slab)
            for m, ref in enumerate((wg, wu)):
                places = pl.ds(pl.multiple_of((2 * core + m) * hidden, hidden), hidden)
                wt[places, rows] = lax.dot_general(
                    ones, ref[core, rows, :], contract_cols, preferred_element_type=f32
                ).astype(bf16)

    transpose(c)

    def transpose_sibling():
        for n, ref in enumerate((wg, wu, wd)):
            arrived(ref.at[1 - c], w_sems + n)
        transpose(1 - c)

    def source_quad(u):
        return rem(k - quad_order[u], nq)

    def rows_of(q):
        return pl.ds(pl.multiple_of(q * quad, quad), quad)

    first_sems = [take(6) for _ in range(nq)]
    last_sems = [take(8) for _ in range(nq)]

    def first_start(u):
        q = source_quad(u)
        for s in range(1 if u == 0 else 0, qz):
            arrived(z_block(q * qz + rem(i - s, qz)), z_sems + u * qz + s)
        for j in (1, 3, 2):
            mine = xg.at[0, y, x, rows_of(q)]
            send(mine, mine, first_sems[u] + j - 1, dev(xx=rem(x + j, NX)))
            mine = xg.at[1, y, x, rows_of(q)]
            send(mine, mine, first_sems[u] + 3 + j - 1, dev(yy=rem(y + j, ny)))

    def t_part(offset, q, part=None):
        cols = pl.ds(0, NX) if part is None else pl.ds(part * (NX // 2), NX // 2)
        return xg.at[0, rem(y + offset + ny, ny), cols, rows_of(q)]

    def g_part(offset, q, part=None):
        cols = pl.ds(0, ny) if part is None else pl.ds(part * (ny // 2), ny // 2)
        return xg.at[1, cols, rem(x + offset + NX, NX), rows_of(q)]

    def last_start(u):
        q = source_quad(u)
        for j in (1, 3, 2):
            arrived(xg.at[0, y, rem(x - j, NX), rows_of(q)], first_sems[u] + j - 1)
        ways = (1, 3, 2) if u in DIRECT else (1, 3)
        for j in ways:
            mine = t_part(0, q)
            send(mine, mine, last_sems[u] + SLOT[j], dev(yy=rem(y + j, ny)))
        for j in (1, 3, 2):
            arrived(xg.at[1, rem(y - j, ny), x, rows_of(q)], first_sems[u] + 3 + j - 1)
        for j in ways:
            mine = g_part(0, q)
            send(mine, mine, last_sems[u] + 4 + SLOT[j], dev(xx=rem(x + j, NX)))

    def last_forward(u):
        if u in DIRECT:
            return
        q = source_quad(u)
        for way in (0, 1):
            step = 1 - 2 * way
            arrived(t_part(-step, q), last_sems[u] + way)
            part = t_part(-step, q, way)
            send(part, part, last_sems[u] + 2 + way, dev(yy=rem(y + step, ny)))
            arrived(g_part(-step, q), last_sems[u] + 4 + way)
            part = g_part(-step, q, way)
            send(part, part, last_sems[u] + 6 + way, dev(xx=rem(x + step, NX)))

    def last_finish(u):
        q = source_quad(u)
        if u in DIRECT:
            for j in (1, 3, 2):
                arrived(t_part(-j, q), last_sems[u] + SLOT[j])
                arrived(g_part(-j, q), last_sems[u] + 4 + SLOT[j])
            return
        for way in (0, 1):
            arrived(t_part(2, q, way), last_sems[u] + 2 + way)
            arrived(g_part(2, q, way), last_sems[u] + 6 + way)

    def product(u):
        q = source_quad(u)
        spans = [
            pl.ds(pl.multiple_of(n * slab + q * quad, quad), quad) for n in range(NX)
        ]

        @pl.loop(0, ny // 2)
        def _(p):
            def rhs(kind):
                return jnp.concatenate(
                    [
                        jnp.concatenate(
                            [xg[kind, 2 * p, n, rows_of(q)], xg[kind, 2 * p + 1, n, rows_of(q)]], axis=1
                        )
                        for n in range(NX)
                    ],
                    axis=0,
                )

            lhs = jnp.concatenate([wt[:, span] for span in spans], axis=1)
            part = jnp.dot(lhs, rhs(0), preferred_element_type=f32)
            pre[p] = part if u == 0 else pre[p] + part
            lhs = jnp.concatenate(
                [jnp.concatenate([wd[m, :, span] for span in spans], axis=1) for m in range(2)], axis=0
            )
            part = jnp.dot(lhs, rhs(1), preferred_element_type=f32)
            hg[p] = part if u == 0 else hg[p] + part

    if nq == 4:
        first_start(0)
        z_start(1)
        z_start(2)
        last_start(0)
        transpose_sibling()
        last_forward(0)
        first_start(1)
        z_start(3)
        first_start(2)
        last_finish(0)
        last_start(1)
        last_start(2)
        first_start(3)
        product(0)
        last_forward(1)
        last_forward(2)
        last_start(3)
        last_finish(1)
        last_finish(2)
        product(1)
        product(2)
        last_forward(3)
        last_finish(3)
        product(3)
    else:
        for u in range(nq):
            if u:
                z_start(u)
            else:
                transpose_sibling()
            first_start(u)
            last_start(u)
            last_forward(u)
            last_finish(u)
            product(u)
    for j in range(1, ny):
        arrived(meta.at[rem(y - j, ny)], meta_sems + j)

    @pl.loop(0, ny // 2)
    def _(p):
        info = jnp.concatenate([meta[2 * p], meta[2 * p + 1]], axis=1)
        sums = [0.0, 0.0]
        for m in range(2):
            rows = 2 * m * hidden
            pre_gate, pre_up = pre[p, rows : rows + hidden], pre[p, rows + hidden : rows + 2 * hidden]
            hidden_grad = hg[p, m * hidden : (m + 1) * hidden]
            mine = (y * 2 + m).astype(f32)
            hit0 = (info[0:1] == mine).astype(f32)
            hit1 = (info[1:2] == mine).astype(f32)
            weight = hit0 * info[2:3] + hit1 * info[3:4]
            s = jax.nn.sigmoid(pre_gate)
            activated = pre_gate * s
            slope = s * (1.0 + pre_gate * (1.0 - s))
            gate_partial = jnp.sum(activated * pre_up * hidden_grad, axis=0, keepdims=True)
            scaled = (weight * activated * pre_up).astype(bf16)
            gate_pre = (weight * hidden_grad * pre_up * slope).astype(bf16)
            up_pre = (weight * hidden_grad * activated).astype(bf16)
            sums[0] += gate_partial * hit0
            sums[1] += gate_partial * hit1
            for n in range(2):
                lanes = slice(n * tokens, (n + 1) * tokens)
                ab[m, 2 * p + n, :hidden] = gate_pre[:, lanes]
                ab[m, 2 * p + n, hidden:] = up_pre[:, lanes]
                hh[m, 2 * p + n] = scaled[:, lanes]
        for n in range(2):
            lanes = slice(n * tokens, (n + 1) * tokens)
            vp[2 * p + n, 0:1] = sums[0][:, lanes]
            vp[2 * p + n, 1:2] = sums[1][:, lanes]

    sum_order = quad_order[::-1]
    s1_sems = [take(6) for _ in range(nq)]
    s2_sems = [take(6) for _ in range(nq)]
    s3_sems = take(nz)

    def target_quad(u):
        return rem(k + sum_order[u], nq)

    def input_grads(u):
        q = target_quad(u)

        @pl.loop(0, ny // 2)
        def _(p):
            spans = [
                pl.ds(pl.multiple_of(n * slab + q * quad, quad), quad) for n in range(NX)
            ]
            weights = jnp.concatenate(
                [
                    jnp.concatenate([wg[0, span], wu[0, span], wg[1, span], wu[1, span]], axis=1)
                    for span in spans
                ],
                axis=0,
            )
            pair = jnp.concatenate(
                [jnp.concatenate([ab[m, 2 * p], ab[m, 2 * p + 1]], axis=1) for m in range(2)], axis=0
            )
            part = jnp.dot(weights, pair, preferred_element_type=f32)
            for n in range(NX):
                for m in range(2):
                    piece = part[n * quad : (n + 1) * quad, m * tokens : (m + 1) * tokens]
                    own[q, 2 * p + m, n] = piece
                    s1[q, 2 * p + m, n] = piece.astype(bf16)

    def first_sum(u):
        q = target_quad(u)
        for j in (2, 1, 3):
            yy, xx = rem(y + j, ny), rem(x + j, NX)
            send(s1.at[q, yy, :, pl.ds(0, half)], r1a.at[q, y], s1_sems[u] + j - 1, dev(yy=yy))
            send(s1.at[q, :, xx, pl.ds(half, half)], r1b.at[q, x], s1_sems[u] + 3 + j - 1, dev(xx=xx))

    def second_sum(u):
        q = target_quad(u)
        for j in (1, 2, 3):
            arrived(r1a.at[q, rem(y - j, ny)], s1_sems[u] + j - 1)
        for j in (2, 1, 3, 0):
            xx = rem(x + j, NX)
            total = own[q, y, xx, :half]
            for m in range(1, ny):
                total += r1a[q, rem(y - m, ny), xx].astype(f32)
            if j:
                s2a[q, xx] = total.astype(bf16)
                send(s2a.at[q, xx], r2a.at[q, x], s2_sems[u] + j - 1, dev(xx=xx))
            else:
                s2fa[q] = total
        for j in (1, 2, 3):
            arrived(r1b.at[q, rem(x - j, NX)], s1_sems[u] + 3 + j - 1)
        for j in (2, 1, 3, 0):
            yy = rem(y + j, ny)
            total = own[q, yy, x, half:]
            for m in range(1, NX):
                total += r1b[q, rem(x - m, NX), yy].astype(f32)
            if j:
                s2b[q, yy] = total.astype(bf16)
                send(s2b.at[q, yy], r2b.at[q, y], s2_sems[u] + 3 + j - 1, dev(yy=yy))
            else:
                s2fb[q] = total

    def third_sum(u):
        q = target_quad(u)
        for j in (1, 2, 3):
            arrived(r2a.at[q, rem(x - j, NX)], s2_sems[u] + j - 1)
        total = s2fa[q]
        for m in range(1, NX):
            total += r2a[q, rem(x - m, NX)].astype(f32)
        s3f[q, :half] = total
        s3[q, :half] = total.astype(bf16)
        for j in (1, 2, 3):
            arrived(r2b.at[q, rem(y - j, ny)], s2_sems[u] + 3 + j - 1)
        total = s2fb[q]
        for m in range(1, ny):
            total += r2b[q, rem(y - m, ny)].astype(f32)
        s3f[q, half:] = total
        s3[q, half:] = total.astype(bf16)
        for s in range(1 if sum_order[u] == 0 else 0, qz):
            place = rem(i + s, qz)
            slot = u * qz + s
            send(s3.at[q, feats(place)], r3.at[slot], s3_sems + slot, dev(zz=q * qz + place))

    gu_sems, d_sems = take(2), take(2)

    def both(ref, core, p):
        return jnp.concatenate([ref[core, 2 * p], ref[core, 2 * p + 1]], axis=1)

    def gate_up_grads(first, last):
        @pl.loop(first, last)
        def _(n):
            total = jnp.zeros((slab, 4 * hidden), f32)
            for p in range(ny // 2):
                lhs = jnp.concatenate([xg[0, 2 * p, n], xg[0, 2 * p + 1, n]], axis=1)
                rhs = jnp.concatenate([both(ab, c, p), both(ab, 1 - c, p)], axis=0)
                total += lax.dot_general(lhs, rhs, contract_cols, preferred_element_type=f32)
            gu_own[n] = total[:, : 2 * hidden]
            gu_out[n] = total[:, 2 * hidden :]

        part = pl.ds(first, last - first)
        send(gu_out.at[part], gu_in.at[part], gu_sems + (1 if first else 0), sibling)

    def down_grads(first, last):
        @pl.loop(first, last)
        def _(n):
            total = jnp.zeros((2 * hidden, slab), f32)
            for p in range(ny // 2):
                lhs = jnp.concatenate([both(hh, c, p), both(hh, 1 - c, p)], axis=0)
                rhs = jnp.concatenate([xg[1, 2 * p, n], xg[1, 2 * p + 1, n]], axis=1)
                total += lax.dot_general(lhs, rhs, contract_cols, preferred_element_type=f32)
            d_own[n] = total[:hidden]
            d_out[n] = total[hidden:]

        part = pl.ds(first, last - first)
        send(d_out.at[part], d_in.at[part], d_sems + (1 if first else 0), sibling)

    def finish_gate_up(first, last):
        arrived(gu_in.at[pl.ds(first, last - first)], gu_sems + (1 if first else 0))

        @pl.loop(first, last)
        def _(n):
            rows = pl.ds(pl.multiple_of(n * slab, slab), slab)
            total = gu_own[n] + gu_in[n]
            og[rows, :] = total[:, :hidden].astype(bf16)
            ou[rows, :] = total[:, hidden:].astype(bf16)

        if last == NX:
            stores[0].start()
            stores[1].start()

    def finish_down(first, last):
        arrived(d_in.at[pl.ds(first, last - first)], d_sems + (1 if first else 0))

        @pl.loop(first, last)
        def _(n):
            rows = pl.ds(pl.multiple_of(n * slab, slab), slab)
            od[:, rows] = (d_own[n] + d_in[n]).astype(bf16)

        if last == NX:
            stores[2].start()

    v_sems, vx_sems, vz_sems = take(ny), take(NX), take(nz)

    def values_start():
        for j in range(1, ny):
            yy = rem(y + j, ny)
            send(vp.at[yy], vr.at[y], v_sems + j, dev(yy=yy))

    def values_x():
        for j in range(1, ny):
            arrived(vr.at[rem(y - j, ny)], v_sems + j)
        vr[y] = vp[y]
        v1[...] = sum(vr[m] for m in range(ny))
        for m in range(1, NX):
            send(v1, vx.at[x], vx_sems + m, dev(xx=rem(x + m, NX)))

    def values_z():
        for m in range(1, NX):
            arrived(vx.at[rem(x - m, NX)], vx_sems + m)
        vx[x] = v1[...]
        vz[z] = sum(vx[m] for m in range(NX))
        for m in range(1, nz):
            send(vz.at[z], vz.at[z], vz_sems + m, dev(zz=rem(z + m, nz)))

    stores = [
        pltpu.make_async_copy(og, ggrad_hbm.at[0], local_sems.at[3]),
        pltpu.make_async_copy(ou, ugrad_hbm.at[0], local_sems.at[4]),
        pltpu.make_async_copy(od, dgrad_hbm.at[0], local_sems.at[5]),
    ]

    if nq == 4:
        input_grads(0)
        first_sum(0)
        values_start()
        input_grads(1)
        first_sum(1)
        input_grads(2)
        input_grads(3)
        first_sum(2)
        values_x()
        drain()
        second_sum(0)
        first_sum(3)
        gate_up_grads(0, NX // 2)
        second_sum(1)
        third_sum(0)
        gate_up_grads(NX // 2, NX)
        values_z()
        second_sum(2)
        third_sum(1)
        down_grads(0, NX // 2)
        finish_gate_up(0, NX // 2)
        finish_gate_up(NX // 2, NX)
        second_sum(3)
        third_sum(2)
        down_grads(NX // 2, NX)
        finish_down(0, NX // 2)
        finish_down(NX // 2, NX)
        third_sum(3)
    else:
        for u in range(nq):
            input_grads(u)
        values_start()
        for u in range(nq):
            first_sum(u)
        values_x()
        gate_up_grads(0, NX // 2)
        gate_up_grads(NX // 2, NX)
        for u in range(nq):
            second_sum(u)
        values_z()
        down_grads(0, NX // 2)
        down_grads(NX // 2, NX)
        finish_gate_up(0, NX // 2)
        finish_gate_up(NX // 2, NX)
        finish_down(0, NX // 2)
        finish_down(NX // 2, NX)
        for u in range(nq):
            third_sum(u)
    drain()

    for m in range(1, nz):
        arrived(vz.at[rem(z - m, nz)], vz_sems + m)
    vgrad_ref[...] = sum(vz[m] for m in range(nz))[0:2]

    result = s3f[k, feats(i)]
    for u in range(nq):
        for s in range(1 if sum_order[u] == 0 else 0, qz):
            slot = u * qz + s
            arrived(r3.at[slot], s3_sems + slot)
            result += r3[slot].astype(f32)
    tgrad_ref[...] = result.astype(bf16)

    for store in stores:
        store.wait()

    drain()
    assert counter[0] <= send_sems.shape[0], counter[0]


def copies(count, *refs):
    sources, targets, held = refs[:count], refs[count : 2 * count], refs[2 * count : 3 * count]
    in_sems, out_sems = refs[3 * count :]
    ins = [pltpu.make_async_copy(sources[n], held[n], in_sems.at[n]) for n in range(count)]
    outs = [pltpu.make_async_copy(held[n], targets[n], out_sems.at[n]) for n in range(count)]
    for move in ins:
        move.start()
    for n in range(count):
        ins[n].wait()
        outs[n].start()
    for move in outs:
        move.wait()


def per_device(tokens, out_grad, routes, gate_values, gate_weight, up_weight, down_weight):
    groups = lax.axis_size("expert")
    ny, nz = groups // 2, lax.axis_size("tensor") // NX
    nq = 4 if nz >= 16 else 2
    count, feat = tokens.shape
    depth, hidden = gate_weight.shape[1:]
    slab, quad = nz * feat, nz // nq * feat
    half = quad // 2
    f32, bf16 = jnp.float32, jnp.bfloat16
    vmem = pl.BlockSpec(memory_space=pltpu.VMEM)
    hbm = pl.BlockSpec(memory_space=pl.ANY)
    scratch = [
        ((2, ny, NX, slab, count), bf16),
        ((ny, 8, count), f32),
        ((2, depth, hidden), bf16),
        ((2, depth, hidden), bf16),
        ((2, hidden, depth), bf16),
        ((4 * hidden, depth), bf16),
        ((ny // 2, 4 * hidden, 2 * count), f32),
        ((ny // 2, 2 * hidden, 2 * count), f32),
        ((2, ny, 2 * hidden, count), bf16),
        ((2, ny, hidden, count), bf16),
        ((nq, ny, NX, quad, count), f32),
        ((nq, ny, NX, quad, count), bf16),
        ((nq, ny, NX, half, count), bf16),
        ((nq, NX, ny, half, count), bf16),
        ((nq, NX, half, count), bf16),
        ((nq, ny, half, count), bf16),
        ((nq, half, count), f32),
        ((nq, half, count), f32),
        ((nq, NX, half, count), bf16),
        ((nq, ny, half, count), bf16),
        ((nq, quad, count), bf16),
        ((nq, quad, count), f32),
        ((nz, feat, count), bf16),
        ((ny, 8, count), f32),
        ((ny, 8, count), f32),
        ((8, count), f32),
        ((NX, 8, count), f32),
        ((nz, 8, count), f32),
        ((depth, hidden), bf16),
        ((depth, hidden), bf16),
        ((hidden, depth), bf16),
        ((NX, slab, 2 * hidden), f32),
        ((NX, slab, 2 * hidden), f32),
        ((NX, slab, 2 * hidden), f32),
        ((NX, hidden, slab), f32),
        ((NX, hidden, slab), f32),
        ((NX, hidden, slab), f32),
        ((2, count), jnp.int32),
        ((2, count), bf16),
    ]
    flops = 2 * groups * count * depth * hidden * 8
    out_shape = (
        jax.ShapeDtypeStruct((feat, count), bf16),
        jax.ShapeDtypeStruct((2, count), f32),
        jax.ShapeDtypeStruct(gate_weight.shape, bf16),
        jax.ShapeDtypeStruct(up_weight.shape, bf16),
        jax.ShapeDtypeStruct(down_weight.shape, bf16),
    )
    results = pl.pallas_call(
        functools.partial(kernel, (ny, nz, nq, feat, count, hidden)),
        out_shape=out_shape,
        in_specs=[hbm] * 7,
        out_specs=(vmem, vmem, hbm, hbm, hbm),
        scratch_shapes=[pltpu.VMEM(shape, dtype) for shape, dtype in scratch]
        + [
            pltpu.SemaphoreType.DMA((280,)),
            pltpu.SemaphoreType.DMA((280,)),
            pltpu.SemaphoreType.DMA((10,)),
        ],
        compiler_params=pltpu.CompilerParams(
            collective_id=0, has_side_effects=True, vmem_limit_bytes=60 * 1024 * 1024
        ),
        cost_estimate=pl.CostEstimate(
            flops=flops, bytes_accessed=2**22, transcendentals=groups * count * hidden
        ),
    )(tokens.T, out_grad.T, routes.T, gate_values.T, gate_weight, up_weight, down_weight)
    tokens_grad, values_grad, *weight_grads = pl.pallas_call(
        functools.partial(copies, len(results)),
        out_shape=out_shape,
        in_specs=[hbm] * len(results),
        out_specs=[hbm] * len(results),
        scratch_shapes=[pltpu.VMEM(result.shape, result.dtype) for result in results]
        + [pltpu.SemaphoreType.DMA((len(results),))] * 2,
        compiler_params=pltpu.CompilerParams(vmem_limit_bytes=60 * 1024 * 1024),
    )(*results)
    return (tokens_grad.T, values_grad.T, *weight_grads)


def solution(mesh):
    in_specs = (
        P("expert", "tensor"),
        P("expert", "tensor"),
        P("expert", None),
        P("expert", None),
        P("expert", None, "tensor"),
        P("expert", None, "tensor"),
        P("expert", "tensor", None),
    )
    out_specs = (
        P("expert", "tensor"),
        P("expert", None),
        P("expert", None, "tensor"),
        P("expert", None, "tensor"),
        P("expert", "tensor", None),
    )
    return jax.shard_map(
        per_device, mesh=mesh, in_specs=in_specs, out_specs=out_specs, check_vma=False
    )
```

```python
import functools

import jax
import jax.numpy as jnp
from jax import lax
from jax.experimental import pallas as pl
from jax.experimental.pallas import tpu as pltpu
from jax.sharding import PartitionSpec as P

MESH = pl.DeviceIdType.MESH
NX = 4
DIRECT = (0, 3)
SLOT = {1: 0, 3: 1, 2: 2}
contract_cols = (((1,), (1,)), ((), ()))


def kernel(
    dims,
    tok_ref, grad_ref, routes_ref, values_ref, gate_hbm, up_hbm, down_hbm,
    tgrad_ref, vgrad_ref, ggrad_hbm, ugrad_hbm, dgrad_hbm,
    xg, meta, wg, wu, wd, wt, pre, hg, ab, hh, own, s1, r1a, r1b,
    s2a, s2b, s2fa, s2fb, r2a, r2b, s3, s3f, r3, vp, vr, v1, vx, vz,
    og, ou, od, gu_own, gu_out, gu_in, d_own, d_out, d_in, rt, vl, send_sems, recv_sems, local_sems,
):
    ny, nz, nq, feat, tokens, hidden = dims
    e = lax.axis_index("expert")
    t = lax.axis_index("tensor")
    y, c = e // 2, e % 2
    x, z = t // nz, t % nz
    qz = nz // nq
    k, i = z // qz, z % qz
    slab = nz * feat
    quad = qz * feat
    half = quad // 2
    groups = 2 * ny
    quad_order = [0, 1, 3, 2][:nq] if nq == 4 else [0, 1]
    f32, bf16 = jnp.float32, jnp.bfloat16

    counter = [0]
    pending = []

    def rem(value, size):
        return lax.rem(value + size, size)

    def dev(xx=None, yy=None, zz=None, cc=None):
        xx = x if xx is None else xx
        yy = y if yy is None else yy
        zz = z if zz is None else zz
        cc = c if cc is None else cc
        return (yy * 2 + cc, xx * nz + zz)

    def take(count=1):
        first = counter[0]
        counter[0] += count
        return first

    def remote(src, dst, index, device):
        return pltpu.make_async_remote_copy(
            src_ref=src, dst_ref=dst, send_sem=send_sems.at[index], recv_sem=recv_sems.at[index],
            device_id=device, device_id_type=MESH,
        )

    def send(src, dst, index, device):
        copy = remote(src, dst, index, device)
        copy.start()
        pending.append(copy)

    def arrived(ref, index):
        remote(ref, ref, index, dev()).wait_recv()

    sibling = dev(cc=1 - c)

    def drain():
        for copy in pending:
            copy.wait_send()
        pending.clear()

    def feats(block):
        return pl.ds(pl.multiple_of(block * feat, feat), feat)

    inputs = [
        pltpu.make_async_copy(tok_ref, xg.at[0, y, x, feats(z)], local_sems.at[6]),
        pltpu.make_async_copy(grad_ref, xg.at[1, y, x, feats(z)], local_sems.at[7]),
        pltpu.make_async_copy(routes_ref, rt, local_sems.at[8]),
        pltpu.make_async_copy(values_ref, vl, local_sems.at[9]),
    ]
    for load in inputs:
        load.start()

    loads = [
        pltpu.make_async_copy(gate_hbm.at[0], wg.at[c], local_sems.at[0]),
        pltpu.make_async_copy(up_hbm.at[0], wu.at[c], local_sems.at[1]),
        pltpu.make_async_copy(down_hbm.at[0], wd.at[c], local_sems.at[2]),
    ]
    for load in loads:
        load.start()

    barrier = pltpu.get_barrier_semaphore()
    for j in range(nz // 2, 0, -1):
        for zz in sorted({j, nz - j}):
            pl.semaphore_signal(barrier, inc=1, device_id=dev(zz=rem(z + zz, nz)), device_id_type=MESH)
    for j in range(1, NX):
        pl.semaphore_signal(barrier, inc=1, device_id=dev(xx=rem(x + j, NX)), device_id_type=MESH)
    for j in range(1, ny):
        pl.semaphore_signal(barrier, inc=1, device_id=dev(yy=rem(y + j, ny)), device_id_type=MESH)
    pl.semaphore_signal(barrier, inc=1, device_id=sibling, device_id_type=MESH)

    for load in inputs:
        load.wait()
    meta[y, 0:2] = rt[...].astype(f32)
    meta[y, 2:4] = vl[...].astype(f32)
    pl.semaphore_wait(barrier, ny - 1 + NX - 1 + nz - 1 + 1)

    def z_block(block):
        return xg.at[:, y, x, feats(block)]

    z_sems = take(nz)

    def z_start(u):
        for s in range(1 if u == 0 else 0, qz):
            zz = rem(k + quad_order[u], nq) * qz + rem(i + s, qz)
            send(z_block(z), z_block(z), z_sems + u * qz + s, dev(zz=zz))

    z_start(0)
    meta_sems = take(ny)
    for j in range(1, ny):
        send(meta.at[y], meta.at[y], meta_sems + j, dev(yy=rem(y + j, ny)))

    for load in loads:
        load.wait()
    w_sems = take(3)
    for n, ref in enumerate((wg, wu, wd)):
        send(ref.at[c], ref.at[c], w_sems + n, sibling)
    ones = (
        lax.broadcasted_iota(jnp.int32, (hidden, hidden), 0)
        == lax.broadcasted_iota(jnp.int32, (hidden, hidden), 1)
    ).astype(bf16)

    def transpose(core):
        @pl.loop(0, NX)
        def _(n):
            rows = pl.ds(pl.multiple_of(n * slab, slab), slab)
            for m, ref in enumerate((wg, wu)):
                places = pl.ds(pl.multiple_of((2 * core + m) * hidden, hidden), hidden)
                wt[places, rows] = lax.dot_general(
                    ones, ref[core, rows, :], contract_cols, preferred_element_type=f32
                ).astype(bf16)

    transpose(c)

    def transpose_sibling():
        for n, ref in enumerate((wg, wu, wd)):
            arrived(ref.at[1 - c], w_sems + n)
        transpose(1 - c)

    def source_quad(u):
        return rem(k - quad_order[u], nq)

    def rows_of(q):
        return pl.ds(pl.multiple_of(q * quad, quad), quad)

    first_sems = [take(6) for _ in range(nq)]
    last_sems = [take(8) for _ in range(nq)]

    def first_start(u):
        q = source_quad(u)
        for s in range(1 if u == 0 else 0, qz):
            arrived(z_block(q * qz + rem(i - s, qz)), z_sems + u * qz + s)
        for j in (1, 3, 2):
            mine = xg.at[0, y, x, rows_of(q)]
            send(mine, mine, first_sems[u] + j - 1, dev(xx=rem(x + j, NX)))
            mine = xg.at[1, y, x, rows_of(q)]
            send(mine, mine, first_sems[u] + 3 + j - 1, dev(yy=rem(y + j, ny)))

    def t_part(offset, q, part=None):
        cols = pl.ds(0, NX) if part is None else pl.ds(part * (NX // 2), NX // 2)
        return xg.at[0, rem(y + offset + ny, ny), cols, rows_of(q)]

    def g_part(offset, q, part=None):
        cols = pl.ds(0, ny) if part is None else pl.ds(part * (ny // 2), ny // 2)
        return xg.at[1, cols, rem(x + offset + NX, NX), rows_of(q)]

    def last_start(u):
        q = source_quad(u)
        for j in (1, 3, 2):
            arrived(xg.at[0, y, rem(x - j, NX), rows_of(q)], first_sems[u] + j - 1)
        ways = (1, 3, 2) if u in DIRECT else (1, 3)
        for j in ways:
            mine = t_part(0, q)
            send(mine, mine, last_sems[u] + SLOT[j], dev(yy=rem(y + j, ny)))
        for j in (1, 3, 2):
            arrived(xg.at[1, rem(y - j, ny), x, rows_of(q)], first_sems[u] + 3 + j - 1)
        for j in ways:
            mine = g_part(0, q)
            send(mine, mine, last_sems[u] + 4 + SLOT[j], dev(xx=rem(x + j, NX)))

    def last_forward(u):
        if u in DIRECT:
            return
        q = source_quad(u)
        for way in (0, 1):
            step = 1 - 2 * way
            arrived(t_part(-step, q), last_sems[u] + way)
            part = t_part(-step, q, way)
            send(part, part, last_sems[u] + 2 + way, dev(yy=rem(y + step, ny)))
            arrived(g_part(-step, q), last_sems[u] + 4 + way)
            part = g_part(-step, q, way)
            send(part, part, last_sems[u] + 6 + way, dev(xx=rem(x + step, NX)))

    def last_finish(u):
        q = source_quad(u)
        if u in DIRECT:
            for j in (1, 3, 2):
                arrived(t_part(-j, q), last_sems[u] + SLOT[j])
                arrived(g_part(-j, q), last_sems[u] + 4 + SLOT[j])
            return
        for way in (0, 1):
            arrived(t_part(2, q, way), last_sems[u] + 2 + way)
            arrived(g_part(2, q, way), last_sems[u] + 6 + way)

    def product(u):
        q = source_quad(u)
        spans = [
            pl.ds(pl.multiple_of(n * slab + q * quad, quad), quad) for n in range(NX)
        ]

        @pl.loop(0, ny // 2)
        def _(p):
            def rhs(kind):
                return jnp.concatenate(
                    [
                        jnp.concatenate(
                            [xg[kind, 2 * p, n, rows_of(q)], xg[kind, 2 * p + 1, n, rows_of(q)]], axis=1
                        )
                        for n in range(NX)
                    ],
                    axis=0,
                )

            lhs = jnp.concatenate([wt[:, span] for span in spans], axis=1)
            part = jnp.dot(lhs, rhs(0), preferred_element_type=f32)
            pre[p] = part if u == 0 else pre[p] + part
            lhs = jnp.concatenate(
                [jnp.concatenate([wd[m, :, span] for span in spans], axis=1) for m in range(2)], axis=0
            )
            part = jnp.dot(lhs, rhs(1), preferred_element_type=f32)
            hg[p] = part if u == 0 else hg[p] + part

    if nq == 4:
        first_start(0)
        z_start(1)
        z_start(2)
        last_start(0)
        transpose_sibling()
        first_start(1)
        z_start(3)
        first_start(2)
        last_forward(0)
        last_start(1)
        last_start(2)
        first_start(3)
        last_finish(0)
        product(0)
        last_forward(1)
        last_forward(2)
        last_start(3)
        last_finish(1)
        last_finish(2)
        product(1)
        product(2)
        last_forward(3)
        last_finish(3)
        product(3)
    else:
        for u in range(nq):
            if u:
                z_start(u)
            else:
                transpose_sibling()
            first_start(u)
            last_start(u)
            last_forward(u)
            last_finish(u)
            product(u)
    for j in range(1, ny):
        arrived(meta.at[rem(y - j, ny)], meta_sems + j)

    @pl.loop(0, ny // 2)
    def _(p):
        info = jnp.concatenate([meta[2 * p], meta[2 * p + 1]], axis=1)
        sums = [0.0, 0.0]
        for m in range(2):
            rows = 2 * m * hidden
            pre_gate, pre_up = pre[p, rows : rows + hidden], pre[p, rows + hidden : rows + 2 * hidden]
            hidden_grad = hg[p, m * hidden : (m + 1) * hidden]
            mine = (y * 2 + m).astype(f32)
            hit0 = (info[0:1] == mine).astype(f32)
            hit1 = (info[1:2] == mine).astype(f32)
            weight = hit0 * info[2:3] + hit1 * info[3:4]
            s = jax.nn.sigmoid(pre_gate)
            activated = pre_gate * s
            slope = s * (1.0 + pre_gate * (1.0 - s))
            gate_partial = jnp.sum(activated * pre_up * hidden_grad, axis=0, keepdims=True)
            scaled = (weight * activated * pre_up).astype(bf16)
            gate_pre = (weight * hidden_grad * pre_up * slope).astype(bf16)
            up_pre = (weight * hidden_grad * activated).astype(bf16)
            sums[0] += gate_partial * hit0
            sums[1] += gate_partial * hit1
            for n in range(2):
                lanes = slice(n * tokens, (n + 1) * tokens)
                ab[m, 2 * p + n, :hidden] = gate_pre[:, lanes]
                ab[m, 2 * p + n, hidden:] = up_pre[:, lanes]
                hh[m, 2 * p + n] = scaled[:, lanes]
        for n in range(2):
            lanes = slice(n * tokens, (n + 1) * tokens)
            vp[2 * p + n, 0:1] = sums[0][:, lanes]
            vp[2 * p + n, 1:2] = sums[1][:, lanes]

    sum_order = quad_order[::-1]
    s1_sems = [take(6) for _ in range(nq)]
    s2_sems = [take(6) for _ in range(nq)]
    s3_sems = take(nz)

    def target_quad(u):
        return rem(k + sum_order[u], nq)

    def input_grads(u):
        q = target_quad(u)

        @pl.loop(0, ny // 2)
        def _(p):
            spans = [
                pl.ds(pl.multiple_of(n * slab + q * quad, quad), quad) for n in range(NX)
            ]
            weights = jnp.concatenate(
                [
                    jnp.concatenate([wg[0, span], wu[0, span], wg[1, span], wu[1, span]], axis=1)
                    for span in spans
                ],
                axis=0,
            )
            pair = jnp.concatenate(
                [jnp.concatenate([ab[m, 2 * p], ab[m, 2 * p + 1]], axis=1) for m in range(2)], axis=0
            )
            part = jnp.dot(weights, pair, preferred_element_type=f32)
            for n in range(NX):
                for m in range(2):
                    piece = part[n * quad : (n + 1) * quad, m * tokens : (m + 1) * tokens]
                    own[q, 2 * p + m, n] = piece
                    s1[q, 2 * p + m, n] = piece.astype(bf16)

    def first_sum(u):
        q = target_quad(u)
        for j in (2, 1, 3):
            yy, xx = rem(y + j, ny), rem(x + j, NX)
            send(s1.at[q, yy, :, pl.ds(0, half)], r1a.at[q, y], s1_sems[u] + j - 1, dev(yy=yy))
            send(s1.at[q, :, xx, pl.ds(half, half)], r1b.at[q, x], s1_sems[u] + 3 + j - 1, dev(xx=xx))

    def second_sum(u):
        q = target_quad(u)
        for j in (1, 2, 3):
            arrived(r1a.at[q, rem(y - j, ny)], s1_sems[u] + j - 1)
        for j in (2, 1, 3, 0):
            xx = rem(x + j, NX)
            total = own[q, y, xx, :half]
            for m in range(1, ny):
                total += r1a[q, rem(y - m, ny), xx].astype(f32)
            if j:
                s2a[q, xx] = total.astype(bf16)
                send(s2a.at[q, xx], r2a.at[q, x], s2_sems[u] + j - 1, dev(xx=xx))
            else:
                s2fa[q] = total
        for j in (1, 2, 3):
            arrived(r1b.at[q, rem(x - j, NX)], s1_sems[u] + 3 + j - 1)
        for j in (2, 1, 3, 0):
            yy = rem(y + j, ny)
            total = own[q, yy, x, half:]
            for m in range(1, NX):
                total += r1b[q, rem(x - m, NX), yy].astype(f32)
            if j:
                s2b[q, yy] = total.astype(bf16)
                send(s2b.at[q, yy], r2b.at[q, y], s2_sems[u] + 3 + j - 1, dev(yy=yy))
            else:
                s2fb[q] = total

    def third_sum(u):
        q = target_quad(u)
        for j in (1, 2, 3):
            arrived(r2a.at[q, rem(x - j, NX)], s2_sems[u] + j - 1)
        total = s2fa[q]
        for m in range(1, NX):
            total += r2a[q, rem(x - m, NX)].astype(f32)
        s3f[q, :half] = total
        s3[q, :half] = total.astype(bf16)
        for j in (1, 2, 3):
            arrived(r2b.at[q, rem(y - j, ny)], s2_sems[u] + 3 + j - 1)
        total = s2fb[q]
        for m in range(1, ny):
            total += r2b[q, rem(y - m, ny)].astype(f32)
        s3f[q, half:] = total
        s3[q, half:] = total.astype(bf16)
        for s in range(1 if sum_order[u] == 0 else 0, qz):
            place = rem(i + s, qz)
            slot = u * qz + s
            send(s3.at[q, feats(place)], r3.at[slot], s3_sems + slot, dev(zz=q * qz + place))

    gu_sems, d_sems = take(2), take(2)

    def both(ref, core, p):
        return jnp.concatenate([ref[core, 2 * p], ref[core, 2 * p + 1]], axis=1)

    def gate_up_grads(first, last):
        @pl.loop(first, last)
        def _(n):
            total = jnp.zeros((slab, 4 * hidden), f32)
            for p in range(ny // 2):
                lhs = jnp.concatenate([xg[0, 2 * p, n], xg[0, 2 * p + 1, n]], axis=1)
                rhs = jnp.concatenate([both(ab, c, p), both(ab, 1 - c, p)], axis=0)
                total += lax.dot_general(lhs, rhs, contract_cols, preferred_element_type=f32)
            gu_own[n] = total[:, : 2 * hidden]
            gu_out[n] = total[:, 2 * hidden :]

        part = pl.ds(first, last - first)
        send(gu_out.at[part], gu_in.at[part], gu_sems + (1 if first else 0), sibling)

    def down_grads(first, last):
        @pl.loop(first, last)
        def _(n):
            total = jnp.zeros((2 * hidden, slab), f32)
            for p in range(ny // 2):
                lhs = jnp.concatenate([both(hh, c, p), both(hh, 1 - c, p)], axis=0)
                rhs = jnp.concatenate([xg[1, 2 * p, n], xg[1, 2 * p + 1, n]], axis=1)
                total += lax.dot_general(lhs, rhs, contract_cols, preferred_element_type=f32)
            d_own[n] = total[:hidden]
            d_out[n] = total[hidden:]

        part = pl.ds(first, last - first)
        send(d_out.at[part], d_in.at[part], d_sems + (1 if first else 0), sibling)

    def finish_gate_up(first, last):
        arrived(gu_in.at[pl.ds(first, last - first)], gu_sems + (1 if first else 0))

        @pl.loop(first, last)
        def _(n):
            rows = pl.ds(pl.multiple_of(n * slab, slab), slab)
            total = gu_own[n] + gu_in[n]
            og[rows, :] = total[:, :hidden].astype(bf16)
            ou[rows, :] = total[:, hidden:].astype(bf16)

        if last == NX:
            stores[0].start()
            stores[1].start()

    def finish_down(first, last):
        arrived(d_in.at[pl.ds(first, last - first)], d_sems + (1 if first else 0))

        @pl.loop(first, last)
        def _(n):
            rows = pl.ds(pl.multiple_of(n * slab, slab), slab)
            od[:, rows] = (d_own[n] + d_in[n]).astype(bf16)

        if last == NX:
            stores[2].start()

    v_sems, vx_sems, vz_sems = take(ny), take(NX), take(nz)

    def values_start():
        for j in range(1, ny):
            yy = rem(y + j, ny)
            send(vp.at[yy], vr.at[y], v_sems + j, dev(yy=yy))

    def values_x():
        for j in range(1, ny):
            arrived(vr.at[rem(y - j, ny)], v_sems + j)
        vr[y] = vp[y]
        v1[...] = sum(vr[m] for m in range(ny))
        for m in range(1, NX):
            send(v1, vx.at[x], vx_sems + m, dev(xx=rem(x + m, NX)))

    def values_z():
        for m in range(1, NX):
            arrived(vx.at[rem(x - m, NX)], vx_sems + m)
        vx[x] = v1[...]
        vz[z] = sum(vx[m] for m in range(NX))
        for m in range(1, nz):
            send(vz.at[z], vz.at[z], vz_sems + m, dev(zz=rem(z + m, nz)))

    stores = [
        pltpu.make_async_copy(og, ggrad_hbm.at[0], local_sems.at[3]),
        pltpu.make_async_copy(ou, ugrad_hbm.at[0], local_sems.at[4]),
        pltpu.make_async_copy(od, dgrad_hbm.at[0], local_sems.at[5]),
    ]

    if nq == 4:
        input_grads(0)
        first_sum(0)
        values_start()
        input_grads(1)
        first_sum(1)
        input_grads(2)
        input_grads(3)
        first_sum(2)
        values_x()
        drain()
        second_sum(0)
        first_sum(3)
        gate_up_grads(0, NX // 2)
        second_sum(1)
        third_sum(0)
        gate_up_grads(NX // 2, NX)
        values_z()
        second_sum(2)
        third_sum(1)
        down_grads(0, NX // 2)
        finish_gate_up(0, NX // 2)
        finish_gate_up(NX // 2, NX)
        second_sum(3)
        third_sum(2)
        down_grads(NX // 2, NX)
        finish_down(0, NX // 2)
        finish_down(NX // 2, NX)
        third_sum(3)
    else:
        for u in range(nq):
            input_grads(u)
        values_start()
        for u in range(nq):
            first_sum(u)
        values_x()
        gate_up_grads(0, NX // 2)
        gate_up_grads(NX // 2, NX)
        for u in range(nq):
            second_sum(u)
        values_z()
        down_grads(0, NX // 2)
        down_grads(NX // 2, NX)
        finish_gate_up(0, NX // 2)
        finish_gate_up(NX // 2, NX)
        finish_down(0, NX // 2)
        finish_down(NX // 2, NX)
        for u in range(nq):
            third_sum(u)
    drain()

    for m in range(1, nz):
        arrived(vz.at[rem(z - m, nz)], vz_sems + m)
    vgrad_ref[...] = sum(vz[m] for m in range(nz))[0:2]

    result = s3f[k, feats(i)]
    for u in range(nq):
        for s in range(1 if sum_order[u] == 0 else 0, qz):
            slot = u * qz + s
            arrived(r3.at[slot], s3_sems + slot)
            result += r3[slot].astype(f32)
    tgrad_ref[...] = result.astype(bf16)

    for store in stores:
        store.wait()

    drain()
    assert counter[0] <= send_sems.shape[0], counter[0]


def copies(count, *refs):
    sources, targets, held = refs[:count], refs[count : 2 * count], refs[2 * count : 3 * count]
    in_sems, out_sems = refs[3 * count :]
    ins = [pltpu.make_async_copy(sources[n], held[n], in_sems.at[n]) for n in range(count)]
    outs = [pltpu.make_async_copy(held[n], targets[n], out_sems.at[n]) for n in range(count)]
    for move in ins:
        move.start()
    for n in range(count):
        ins[n].wait()
        outs[n].start()
    for move in outs:
        move.wait()


def per_device(tokens, out_grad, routes, gate_values, gate_weight, up_weight, down_weight):
    groups = lax.axis_size("expert")
    ny, nz = groups // 2, lax.axis_size("tensor") // NX
    nq = 4 if nz >= 16 else 2
    count, feat = tokens.shape
    depth, hidden = gate_weight.shape[1:]
    slab, quad = nz * feat, nz // nq * feat
    half = quad // 2
    f32, bf16 = jnp.float32, jnp.bfloat16
    vmem = pl.BlockSpec(memory_space=pltpu.VMEM)
    hbm = pl.BlockSpec(memory_space=pl.ANY)
    scratch = [
        ((2, ny, NX, slab, count), bf16),
        ((ny, 8, count), f32),
        ((2, depth, hidden), bf16),
        ((2, depth, hidden), bf16),
        ((2, hidden, depth), bf16),
        ((4 * hidden, depth), bf16),
        ((ny // 2, 4 * hidden, 2 * count), f32),
        ((ny // 2, 2 * hidden, 2 * count), f32),
        ((2, ny, 2 * hidden, count), bf16),
        ((2, ny, hidden, count), bf16),
        ((nq, ny, NX, quad, count), f32),
        ((nq, ny, NX, quad, count), bf16),
        ((nq, ny, NX, half, count), bf16),
        ((nq, NX, ny, half, count), bf16),
        ((nq, NX, half, count), bf16),
        ((nq, ny, half, count), bf16),
        ((nq, half, count), f32),
        ((nq, half, count), f32),
        ((nq, NX, half, count), bf16),
        ((nq, ny, half, count), bf16),
        ((nq, quad, count), bf16),
        ((nq, quad, count), f32),
        ((nz, feat, count), bf16),
        ((ny, 8, count), f32),
        ((ny, 8, count), f32),
        ((8, count), f32),
        ((NX, 8, count), f32),
        ((nz, 8, count), f32),
        ((depth, hidden), bf16),
        ((depth, hidden), bf16),
        ((hidden, depth), bf16),
        ((NX, slab, 2 * hidden), f32),
        ((NX, slab, 2 * hidden), f32),
        ((NX, slab, 2 * hidden), f32),
        ((NX, hidden, slab), f32),
        ((NX, hidden, slab), f32),
        ((NX, hidden, slab), f32),
        ((2, count), jnp.int32),
        ((2, count), bf16),
    ]
    flops = 2 * groups * count * depth * hidden * 8
    out_shape = (
        jax.ShapeDtypeStruct((feat, count), bf16),
        jax.ShapeDtypeStruct((2, count), f32),
        jax.ShapeDtypeStruct(gate_weight.shape, bf16),
        jax.ShapeDtypeStruct(up_weight.shape, bf16),
        jax.ShapeDtypeStruct(down_weight.shape, bf16),
    )
    results = pl.pallas_call(
        functools.partial(kernel, (ny, nz, nq, feat, count, hidden)),
        out_shape=out_shape,
        in_specs=[hbm] * 7,
        out_specs=(vmem, vmem, hbm, hbm, hbm),
        scratch_shapes=[pltpu.VMEM(shape, dtype) for shape, dtype in scratch]
        + [
            pltpu.SemaphoreType.DMA((280,)),
            pltpu.SemaphoreType.DMA((280,)),
            pltpu.SemaphoreType.DMA((10,)),
        ],
        compiler_params=pltpu.CompilerParams(
            collective_id=0, has_side_effects=True, vmem_limit_bytes=60 * 1024 * 1024
        ),
        cost_estimate=pl.CostEstimate(
            flops=flops, bytes_accessed=2**22, transcendentals=groups * count * hidden
        ),
    )(tokens.T, out_grad.T, routes.T, gate_values.T, gate_weight, up_weight, down_weight)
    tokens_grad, values_grad, *weight_grads = pl.pallas_call(
        functools.partial(copies, len(results)),
        out_shape=out_shape,
        in_specs=[hbm] * len(results),
        out_specs=[hbm] * len(results),
        scratch_shapes=[pltpu.VMEM(result.shape, result.dtype) for result in results]
        + [pltpu.SemaphoreType.DMA((len(results),))] * 2,
        compiler_params=pltpu.CompilerParams(vmem_limit_bytes=60 * 1024 * 1024),
    )(*results)
    return (tokens_grad.T, values_grad.T, *weight_grads)


def solution(mesh):
    in_specs = (
        P("expert", "tensor"),
        P("expert", "tensor"),
        P("expert", None),
        P("expert", None),
        P("expert", None, "tensor"),
        P("expert", None, "tensor"),
        P("expert", "tensor", None),
    )
    out_specs = (
        P("expert", "tensor"),
        P("expert", None),
        P("expert", None, "tensor"),
        P("expert", None, "tensor"),
        P("expert", "tensor", None),
    )
    return jax.shard_map(
        per_device, mesh=mesh, in_specs=in_specs, out_specs=out_specs, check_vma=False
    )
```

```python
import functools

import jax
import jax.numpy as jnp
from jax import lax
from jax.experimental import pallas as pl
from jax.experimental.pallas import tpu as pltpu
from jax.sharding import PartitionSpec as P

MESH = pl.DeviceIdType.MESH
NX = 4
DIRECT = (0, 3)
SLOT = {1: 0, 3: 1, 2: 2}
contract_cols = (((1,), (1,)), ((), ()))


def kernel(
    dims,
    tok_ref, grad_ref, routes_ref, values_ref, gate_hbm, up_hbm, down_hbm,
    tgrad_ref, vgrad_ref, ggrad_hbm, ugrad_hbm, dgrad_hbm,
    xg, meta, wg, wu, wd, wt, pre, hg, ab, hh, own, s1, r1a, r1b,
    s2a, s2b, s2fa, s2fb, r2a, r2b, s3, s3f, r3, vp, vr, v1, vx, vz,
    og, ou, od, gu_own, gu_out, gu_in, d_own, d_out, d_in, rt, vl, send_sems, recv_sems, local_sems,
):
    ny, nz, nq, feat, tokens, hidden = dims
    e = lax.axis_index("expert")
    t = lax.axis_index("tensor")
    y, c = e // 2, e % 2
    x, z = t // nz, t % nz
    qz = nz // nq
    k, i = z // qz, z % qz
    slab = nz * feat
    quad = qz * feat
    half = quad // 2
    groups = 2 * ny
    quad_order = [0, 1, 3, 2][:nq] if nq == 4 else [0, 1]
    f32, bf16 = jnp.float32, jnp.bfloat16

    counter = [0]
    pending = []

    def rem(value, size):
        return lax.rem(value + size, size)

    def dev(xx=None, yy=None, zz=None, cc=None):
        xx = x if xx is None else xx
        yy = y if yy is None else yy
        zz = z if zz is None else zz
        cc = c if cc is None else cc
        return (yy * 2 + cc, xx * nz + zz)

    def take(count=1):
        first = counter[0]
        counter[0] += count
        return first

    def remote(src, dst, index, device):
        return pltpu.make_async_remote_copy(
            src_ref=src, dst_ref=dst, send_sem=send_sems.at[index], recv_sem=recv_sems.at[index],
            device_id=device, device_id_type=MESH,
        )

    def send(src, dst, index, device):
        copy = remote(src, dst, index, device)
        copy.start()
        pending.append(copy)

    def arrived(ref, index):
        remote(ref, ref, index, dev()).wait_recv()

    sibling = dev(cc=1 - c)

    def drain():
        for copy in pending:
            copy.wait_send()
        pending.clear()

    def feats(block):
        return pl.ds(pl.multiple_of(block * feat, feat), feat)

    inputs = [
        pltpu.make_async_copy(tok_ref, xg.at[0, y, x, feats(z)], local_sems.at[6]),
        pltpu.make_async_copy(grad_ref, xg.at[1, y, x, feats(z)], local_sems.at[7]),
        pltpu.make_async_copy(routes_ref, rt, local_sems.at[8]),
        pltpu.make_async_copy(values_ref, vl, local_sems.at[9]),
    ]
    for load in inputs:
        load.start()

    loads = [
        pltpu.make_async_copy(gate_hbm.at[0], wg.at[c], local_sems.at[0]),
        pltpu.make_async_copy(up_hbm.at[0], wu.at[c], local_sems.at[1]),
        pltpu.make_async_copy(down_hbm.at[0], wd.at[c], local_sems.at[2]),
    ]
    for load in loads:
        load.start()

    barrier = pltpu.get_barrier_semaphore()
    for j in range(nz // 2, 0, -1):
        for zz in sorted({j, nz - j}):
            pl.semaphore_signal(barrier, inc=1, device_id=dev(zz=rem(z + zz, nz)), device_id_type=MESH)
    for j in range(1, NX):
        pl.semaphore_signal(barrier, inc=1, device_id=dev(xx=rem(x + j, NX)), device_id_type=MESH)
    for j in range(1, ny):
        pl.semaphore_signal(barrier, inc=1, device_id=dev(yy=rem(y + j, ny)), device_id_type=MESH)
    pl.semaphore_signal(barrier, inc=1, device_id=sibling, device_id_type=MESH)

    for load in inputs:
        load.wait()
    meta[y, 0:2] = rt[...].astype(f32)
    meta[y, 2:4] = vl[...].astype(f32)
    pl.semaphore_wait(barrier, ny - 1 + NX - 1 + nz - 1 + 1)

    def z_block(block):
        return xg.at[:, y, x, feats(block)]

    z_sems = take(nz)

    def z_start(u):
        for s in range(1 if u == 0 else 0, qz):
            zz = rem(k + quad_order[u], nq) * qz + rem(i + s, qz)
            send(z_block(z), z_block(z), z_sems + u * qz + s, dev(zz=zz))

    z_start(0)
    meta_sems = take(ny)
    for j in range(1, ny):
        send(meta.at[y], meta.at[y], meta_sems + j, dev(yy=rem(y + j, ny)))

    for load in loads:
        load.wait()
    w_sems = take(3)
    for n, ref in enumerate((wg, wu, wd)):
        send(ref.at[c], ref.at[c], w_sems + n, sibling)
    ones = (
        lax.broadcasted_iota(jnp.int32, (hidden, hidden), 0)
        == lax.broadcasted_iota(jnp.int32, (hidden, hidden), 1)
    ).astype(bf16)

    def transpose(core):
        @pl.loop(0, NX)
        def _(n):
            rows = pl.ds(pl.multiple_of(n * slab, slab), slab)
            for m, ref in enumerate((wg, wu)):
                places = pl.ds(pl.multiple_of((2 * core + m) * hidden, hidden), hidden)
                wt[places, rows] = lax.dot_general(
                    ones, ref[core, rows, :], contract_cols, preferred_element_type=f32
                ).astype(bf16)

    transpose(c)

    def transpose_sibling():
        for n, ref in enumerate((wg, wu, wd)):
            arrived(ref.at[1 - c], w_sems + n)
        transpose(1 - c)

    def source_quad(u):
        return rem(k - quad_order[u], nq)

    def rows_of(q):
        return pl.ds(pl.multiple_of(q * quad, quad), quad)

    first_sems = [take(6) for _ in range(nq)]
    last_sems = [take(8) for _ in range(nq)]

    def first_start(u):
        q = source_quad(u)
        for s in range(1 if u == 0 else 0, qz):
            arrived(z_block(q * qz + rem(i - s, qz)), z_sems + u * qz + s)
        for j in (1, 3, 2):
            mine = xg.at[0, y, x, rows_of(q)]
            send(mine, mine, first_sems[u] + j - 1, dev(xx=rem(x + j, NX)))
            mine = xg.at[1, y, x, rows_of(q)]
            send(mine, mine, first_sems[u] + 3 + j - 1, dev(yy=rem(y + j, ny)))

    def t_part(offset, q, part=None):
        cols = pl.ds(0, NX) if part is None else pl.ds(part * (NX // 2), NX // 2)
        return xg.at[0, rem(y + offset + ny, ny), cols, rows_of(q)]

    def g_part(offset, q, part=None):
        cols = pl.ds(0, ny) if part is None else pl.ds(part * (ny // 2), ny // 2)
        return xg.at[1, cols, rem(x + offset + NX, NX), rows_of(q)]

    def last_start(u):
        q = source_quad(u)
        for j in (1, 3, 2):
            arrived(xg.at[0, y, rem(x - j, NX), rows_of(q)], first_sems[u] + j - 1)
        ways = (1, 3, 2) if u in DIRECT else (1, 3)
        for j in ways:
            mine = t_part(0, q)
            send(mine, mine, last_sems[u] + SLOT[j], dev(yy=rem(y + j, ny)))
        for j in (1, 3, 2):
            arrived(xg.at[1, rem(y - j, ny), x, rows_of(q)], first_sems[u] + 3 + j - 1)
        for j in ways:
            mine = g_part(0, q)
            send(mine, mine, last_sems[u] + 4 + SLOT[j], dev(xx=rem(x + j, NX)))

    def last_forward(u):
        if u in DIRECT:
            return
        q = source_quad(u)
        for way in (0, 1):
            step = 1 - 2 * way
            arrived(t_part(-step, q), last_sems[u] + way)
            part = t_part(-step, q, way)
            send(part, part, last_sems[u] + 2 + way, dev(yy=rem(y + step, ny)))
            arrived(g_part(-step, q), last_sems[u] + 4 + way)
            part = g_part(-step, q, way)
            send(part, part, last_sems[u] + 6 + way, dev(xx=rem(x + step, NX)))

    def last_finish(u):
        q = source_quad(u)
        if u in DIRECT:
            for j in (1, 3, 2):
                arrived(t_part(-j, q), last_sems[u] + SLOT[j])
                arrived(g_part(-j, q), last_sems[u] + 4 + SLOT[j])
            return
        for way in (0, 1):
            arrived(t_part(2, q, way), last_sems[u] + 2 + way)
            arrived(g_part(2, q, way), last_sems[u] + 6 + way)

    def product(u):
        q = source_quad(u)
        spans = [
            pl.ds(pl.multiple_of(n * slab + q * quad, quad), quad) for n in range(NX)
        ]

        @pl.loop(0, ny // 2)
        def _(p):
            def rhs(kind):
                return jnp.concatenate(
                    [
                        jnp.concatenate(
                            [xg[kind, 2 * p, n, rows_of(q)], xg[kind, 2 * p + 1, n, rows_of(q)]], axis=1
                        )
                        for n in range(NX)
                    ],
                    axis=0,
                )

            lhs = jnp.concatenate([wt[:, span] for span in spans], axis=1)
            part = jnp.dot(lhs, rhs(0), preferred_element_type=f32)
            pre[p] = part if u == 0 else pre[p] + part
            lhs = jnp.concatenate(
                [jnp.concatenate([wd[m, :, span] for span in spans], axis=1) for m in range(2)], axis=0
            )
            part = jnp.dot(lhs, rhs(1), preferred_element_type=f32)
            hg[p] = part if u == 0 else hg[p] + part

    if nq == 4:
        first_start(0)
        z_start(1)
        z_start(2)
        last_start(0)
        transpose_sibling()
        first_start(1)
        z_start(3)
        first_start(2)
        last_forward(0)
        last_start(1)
        last_start(2)
        first_start(3)
        last_finish(0)
        product(0)
        last_forward(1)
        last_forward(2)
        last_start(3)
        last_finish(1)
        last_finish(2)
        product(1)
        product(2)
        last_forward(3)
        last_finish(3)
        product(3)
    else:
        for u in range(nq):
            if u:
                z_start(u)
            else:
                transpose_sibling()
            first_start(u)
            last_start(u)
            last_forward(u)
            last_finish(u)
            product(u)
    for j in range(1, ny):
        arrived(meta.at[rem(y - j, ny)], meta_sems + j)

    @pl.loop(0, ny // 2)
    def _(p):
        info = jnp.concatenate([meta[2 * p], meta[2 * p + 1]], axis=1)
        sums = [0.0, 0.0]
        for m in range(2):
            rows = 2 * m * hidden
            pre_gate, pre_up = pre[p, rows : rows + hidden], pre[p, rows + hidden : rows + 2 * hidden]
            hidden_grad = hg[p, m * hidden : (m + 1) * hidden]
            mine = (y * 2 + m).astype(f32)
            hit0 = (info[0:1] == mine).astype(f32)
            hit1 = (info[1:2] == mine).astype(f32)
            weight = hit0 * info[2:3] + hit1 * info[3:4]
            s = jax.nn.sigmoid(pre_gate)
            activated = pre_gate * s
            slope = s * (1.0 + pre_gate * (1.0 - s))
            gate_partial = jnp.sum(activated * pre_up * hidden_grad, axis=0, keepdims=True)
            scaled = (weight * activated * pre_up).astype(bf16)
            gate_pre = (weight * hidden_grad * pre_up * slope).astype(bf16)
            up_pre = (weight * hidden_grad * activated).astype(bf16)
            sums[0] += gate_partial * hit0
            sums[1] += gate_partial * hit1
            for n in range(2):
                lanes = slice(n * tokens, (n + 1) * tokens)
                ab[m, 2 * p + n, :hidden] = gate_pre[:, lanes]
                ab[m, 2 * p + n, hidden:] = up_pre[:, lanes]
                hh[m, 2 * p + n] = scaled[:, lanes]
        for n in range(2):
            lanes = slice(n * tokens, (n + 1) * tokens)
            vp[2 * p + n, 0:1] = sums[0][:, lanes]
            vp[2 * p + n, 1:2] = sums[1][:, lanes]

    sum_order = quad_order[::-1]
    s1_sems = [take(6) for _ in range(nq)]
    s2_sems = [take(6) for _ in range(nq)]
    s3_sems = take(nz)

    def target_quad(u):
        return rem(k + sum_order[u], nq)

    def input_grads(u):
        q = target_quad(u)

        @pl.loop(0, ny // 2)
        def _(p):
            spans = [
                pl.ds(pl.multiple_of(n * slab + q * quad, quad), quad) for n in range(NX)
            ]
            weights = jnp.concatenate(
                [
                    jnp.concatenate([wg[0, span], wu[0, span], wg[1, span], wu[1, span]], axis=1)
                    for span in spans
                ],
                axis=0,
            )
            pair = jnp.concatenate(
                [jnp.concatenate([ab[m, 2 * p], ab[m, 2 * p + 1]], axis=1) for m in range(2)], axis=0
            )
            part = jnp.dot(weights, pair, preferred_element_type=f32)
            for n in range(NX):
                for m in range(2):
                    piece = part[n * quad : (n + 1) * quad, m * tokens : (m + 1) * tokens]
                    s1[q, 2 * p + m, n] = piece.astype(bf16)

                    @pl.when(2 * p + m == y)
                    def _():
                        own[q, 2 * p + m, n, :half] = piece[:half]

                    @pl.when(x == n)
                    def _():
                        own[q, 2 * p + m, n, half:] = piece[half:]

    def first_sum(u):
        q = target_quad(u)
        for j in (2, 1, 3):
            yy, xx = rem(y + j, ny), rem(x + j, NX)
            send(s1.at[q, yy, :, pl.ds(0, half)], r1a.at[q, y], s1_sems[u] + j - 1, dev(yy=yy))
            send(s1.at[q, :, xx, pl.ds(half, half)], r1b.at[q, x], s1_sems[u] + 3 + j - 1, dev(xx=xx))

    def second_sum(u):
        q = target_quad(u)
        for j in (1, 2, 3):
            arrived(r1a.at[q, rem(y - j, ny)], s1_sems[u] + j - 1)
        for j in (2, 1, 3, 0):
            xx = rem(x + j, NX)
            total = own[q, y, xx, :half]
            for m in range(1, ny):
                total += r1a[q, rem(y - m, ny), xx].astype(f32)
            if j:
                s2a[q, xx] = total.astype(bf16)
                send(s2a.at[q, xx], r2a.at[q, x], s2_sems[u] + j - 1, dev(xx=xx))
            else:
                s2fa[q] = total
        for j in (1, 2, 3):
            arrived(r1b.at[q, rem(x - j, NX)], s1_sems[u] + 3 + j - 1)
        for j in (2, 1, 3, 0):
            yy = rem(y + j, ny)
            total = own[q, yy, x, half:]
            for m in range(1, NX):
                total += r1b[q, rem(x - m, NX), yy].astype(f32)
            if j:
                s2b[q, yy] = total.astype(bf16)
                send(s2b.at[q, yy], r2b.at[q, y], s2_sems[u] + 3 + j - 1, dev(yy=yy))
            else:
                s2fb[q] = total

    def third_sum(u):
        q = target_quad(u)
        for j in (1, 2, 3):
            arrived(r2a.at[q, rem(x - j, NX)], s2_sems[u] + j - 1)
        total = s2fa[q]
        for m in range(1, NX):
            total += r2a[q, rem(x - m, NX)].astype(f32)
        s3f[q, :half] = total
        s3[q, :half] = total.astype(bf16)
        for j in (1, 2, 3):
            arrived(r2b.at[q, rem(y - j, ny)], s2_sems[u] + 3 + j - 1)
        total = s2fb[q]
        for m in range(1, ny):
            total += r2b[q, rem(y - m, ny)].astype(f32)
        s3f[q, half:] = total
        s3[q, half:] = total.astype(bf16)
        for s in range(1 if sum_order[u] == 0 else 0, qz):
            place = rem(i + s, qz)
            slot = u * qz + s
            send(s3.at[q, feats(place)], r3.at[slot], s3_sems + slot, dev(zz=q * qz + place))

    gu_sems, d_sems = take(2), take(2)

    def both(ref, core, p):
        return jnp.concatenate([ref[core, 2 * p], ref[core, 2 * p + 1]], axis=1)

    def gate_up_grads(first, last):
        @pl.loop(first, last)
        def _(n):
            total = jnp.zeros((slab, 4 * hidden), f32)
            for p in range(ny // 2):
                lhs = jnp.concatenate([xg[0, 2 * p, n], xg[0, 2 * p + 1, n]], axis=1)
                rhs = jnp.concatenate([both(ab, c, p), both(ab, 1 - c, p)], axis=0)
                total += lax.dot_general(lhs, rhs, contract_cols, preferred_element_type=f32)
            gu_own[n] = total[:, : 2 * hidden]
            gu_out[n] = total[:, 2 * hidden :]

        part = pl.ds(first, last - first)
        send(gu_out.at[part], gu_in.at[part], gu_sems + (1 if first else 0), sibling)

    def down_grads(first, last):
        @pl.loop(first, last)
        def _(n):
            total = jnp.zeros((2 * hidden, slab), f32)
            for p in range(ny // 2):
                lhs = jnp.concatenate([both(hh, c, p), both(hh, 1 - c, p)], axis=0)
                rhs = jnp.concatenate([xg[1, 2 * p, n], xg[1, 2 * p + 1, n]], axis=1)
                total += lax.dot_general(lhs, rhs, contract_cols, preferred_element_type=f32)
            d_own[n] = total[:hidden]
            d_out[n] = total[hidden:]

        part = pl.ds(first, last - first)
        send(d_out.at[part], d_in.at[part], d_sems + (1 if first else 0), sibling)

    def finish_gate_up(first, last):
        arrived(gu_in.at[pl.ds(first, last - first)], gu_sems + (1 if first else 0))

        @pl.loop(first, last)
        def _(n):
            rows = pl.ds(pl.multiple_of(n * slab, slab), slab)
            total = gu_own[n] + gu_in[n]
            og[rows, :] = total[:, :hidden].astype(bf16)
            ou[rows, :] = total[:, hidden:].astype(bf16)

        if last == NX:
            stores[0].start()
            stores[1].start()

    def finish_down(first, last):
        arrived(d_in.at[pl.ds(first, last - first)], d_sems + (1 if first else 0))

        @pl.loop(first, last)
        def _(n):
            rows = pl.ds(pl.multiple_of(n * slab, slab), slab)
            od[:, rows] = (d_own[n] + d_in[n]).astype(bf16)

        if last == NX:
            stores[2].start()

    v_sems, vx_sems, vz_sems = take(ny), take(NX), take(nz)

    def values_start():
        for j in range(1, ny):
            yy = rem(y + j, ny)
            send(vp.at[yy], vr.at[y], v_sems + j, dev(yy=yy))

    def values_x():
        for j in range(1, ny):
            arrived(vr.at[rem(y - j, ny)], v_sems + j)
        vr[y] = vp[y]
        v1[...] = sum(vr[m] for m in range(ny))
        for m in range(1, NX):
            send(v1, vx.at[x], vx_sems + m, dev(xx=rem(x + m, NX)))

    def values_z():
        for m in range(1, NX):
            arrived(vx.at[rem(x - m, NX)], vx_sems + m)
        vx[x] = v1[...]
        vz[z] = sum(vx[m] for m in range(NX))
        for m in range(1, nz):
            send(vz.at[z], vz.at[z], vz_sems + m, dev(zz=rem(z + m, nz)))

    stores = [
        pltpu.make_async_copy(og, ggrad_hbm.at[0], local_sems.at[3]),
        pltpu.make_async_copy(ou, ugrad_hbm.at[0], local_sems.at[4]),
        pltpu.make_async_copy(od, dgrad_hbm.at[0], local_sems.at[5]),
    ]

    if nq == 4:
        input_grads(0)
        first_sum(0)
        values_start()
        input_grads(1)
        first_sum(1)
        input_grads(2)
        input_grads(3)
        first_sum(2)
        values_x()
        drain()
        second_sum(0)
        first_sum(3)
        gate_up_grads(0, NX // 2)
        second_sum(1)
        third_sum(0)
        gate_up_grads(NX // 2, NX)
        values_z()
        second_sum(2)
        third_sum(1)
        down_grads(0, NX // 2)
        finish_gate_up(0, NX // 2)
        finish_gate_up(NX // 2, NX)
        second_sum(3)
        third_sum(2)
        down_grads(NX // 2, NX)
        finish_down(0, NX // 2)
        finish_down(NX // 2, NX)
        third_sum(3)
    else:
        for u in range(nq):
            input_grads(u)
        values_start()
        for u in range(nq):
            first_sum(u)
        values_x()
        gate_up_grads(0, NX // 2)
        gate_up_grads(NX // 2, NX)
        for u in range(nq):
            second_sum(u)
        values_z()
        down_grads(0, NX // 2)
        down_grads(NX // 2, NX)
        finish_gate_up(0, NX // 2)
        finish_gate_up(NX // 2, NX)
        finish_down(0, NX // 2)
        finish_down(NX // 2, NX)
        for u in range(nq):
            third_sum(u)
    drain()

    for m in range(1, nz):
        arrived(vz.at[rem(z - m, nz)], vz_sems + m)
    vgrad_ref[...] = sum(vz[m] for m in range(nz))[0:2]

    result = s3f[k, feats(i)]
    for u in range(nq):
        for s in range(1 if sum_order[u] == 0 else 0, qz):
            slot = u * qz + s
            arrived(r3.at[slot], s3_sems + slot)
            result += r3[slot].astype(f32)
    tgrad_ref[...] = result.astype(bf16)

    for store in stores:
        store.wait()

    drain()
    assert counter[0] <= send_sems.shape[0], counter[0]


def copies(count, *refs):
    sources, targets, held = refs[:count], refs[count : 2 * count], refs[2 * count : 3 * count]
    in_sems, out_sems = refs[3 * count :]
    ins = [pltpu.make_async_copy(sources[n], held[n], in_sems.at[n]) for n in range(count)]
    outs = [pltpu.make_async_copy(held[n], targets[n], out_sems.at[n]) for n in range(count)]
    for move in ins:
        move.start()
    for n in range(count):
        ins[n].wait()
        outs[n].start()
    for move in outs:
        move.wait()


def per_device(tokens, out_grad, routes, gate_values, gate_weight, up_weight, down_weight):
    groups = lax.axis_size("expert")
    ny, nz = groups // 2, lax.axis_size("tensor") // NX
    nq = 4 if nz >= 16 else 2
    count, feat = tokens.shape
    depth, hidden = gate_weight.shape[1:]
    slab, quad = nz * feat, nz // nq * feat
    half = quad // 2
    f32, bf16 = jnp.float32, jnp.bfloat16
    vmem = pl.BlockSpec(memory_space=pltpu.VMEM)
    hbm = pl.BlockSpec(memory_space=pl.ANY)
    scratch = [
        ((2, ny, NX, slab, count), bf16),
        ((ny, 8, count), f32),
        ((2, depth, hidden), bf16),
        ((2, depth, hidden), bf16),
        ((2, hidden, depth), bf16),
        ((4 * hidden, depth), bf16),
        ((ny // 2, 4 * hidden, 2 * count), f32),
        ((ny // 2, 2 * hidden, 2 * count), f32),
        ((2, ny, 2 * hidden, count), bf16),
        ((2, ny, hidden, count), bf16),
        ((nq, ny, NX, quad, count), f32),
        ((nq, ny, NX, quad, count), bf16),
        ((nq, ny, NX, half, count), bf16),
        ((nq, NX, ny, half, count), bf16),
        ((nq, NX, half, count), bf16),
        ((nq, ny, half, count), bf16),
        ((nq, half, count), f32),
        ((nq, half, count), f32),
        ((nq, NX, half, count), bf16),
        ((nq, ny, half, count), bf16),
        ((nq, quad, count), bf16),
        ((nq, quad, count), f32),
        ((nz, feat, count), bf16),
        ((ny, 8, count), f32),
        ((ny, 8, count), f32),
        ((8, count), f32),
        ((NX, 8, count), f32),
        ((nz, 8, count), f32),
        ((depth, hidden), bf16),
        ((depth, hidden), bf16),
        ((hidden, depth), bf16),
        ((NX, slab, 2 * hidden), f32),
        ((NX, slab, 2 * hidden), f32),
        ((NX, slab, 2 * hidden), f32),
        ((NX, hidden, slab), f32),
        ((NX, hidden, slab), f32),
        ((NX, hidden, slab), f32),
        ((2, count), jnp.int32),
        ((2, count), bf16),
    ]
    flops = 2 * groups * count * depth * hidden * 8
    out_shape = (
        jax.ShapeDtypeStruct((feat, count), bf16),
        jax.ShapeDtypeStruct((2, count), f32),
        jax.ShapeDtypeStruct(gate_weight.shape, bf16),
        jax.ShapeDtypeStruct(up_weight.shape, bf16),
        jax.ShapeDtypeStruct(down_weight.shape, bf16),
    )
    results = pl.pallas_call(
        functools.partial(kernel, (ny, nz, nq, feat, count, hidden)),
        out_shape=out_shape,
        in_specs=[hbm] * 7,
        out_specs=(vmem, vmem, hbm, hbm, hbm),
        scratch_shapes=[pltpu.VMEM(shape, dtype) for shape, dtype in scratch]
        + [
            pltpu.SemaphoreType.DMA((280,)),
            pltpu.SemaphoreType.DMA((280,)),
            pltpu.SemaphoreType.DMA((10,)),
        ],
        compiler_params=pltpu.CompilerParams(
            collective_id=0, has_side_effects=True, vmem_limit_bytes=60 * 1024 * 1024
        ),
        cost_estimate=pl.CostEstimate(
            flops=flops, bytes_accessed=2**22, transcendentals=groups * count * hidden
        ),
    )(tokens.T, out_grad.T, routes.T, gate_values.T, gate_weight, up_weight, down_weight)
    tokens_grad, values_grad, *weight_grads = pl.pallas_call(
        functools.partial(copies, len(results)),
        out_shape=out_shape,
        in_specs=[hbm] * len(results),
        out_specs=[hbm] * len(results),
        scratch_shapes=[pltpu.VMEM(result.shape, result.dtype) for result in results]
        + [pltpu.SemaphoreType.DMA((len(results),))] * 2,
        compiler_params=pltpu.CompilerParams(vmem_limit_bytes=60 * 1024 * 1024),
    )(*results)
    return (tokens_grad.T, values_grad.T, *weight_grads)


def solution(mesh):
    in_specs = (
        P("expert", "tensor"),
        P("expert", "tensor"),
        P("expert", None),
        P("expert", None),
        P("expert", None, "tensor"),
        P("expert", None, "tensor"),
        P("expert", "tensor", None),
    )
    out_specs = (
        P("expert", "tensor"),
        P("expert", None),
        P("expert", None, "tensor"),
        P("expert", None, "tensor"),
        P("expert", "tensor", None),
    )
    return jax.shard_map(
        per_device, mesh=mesh, in_specs=in_specs, out_specs=out_specs, check_vma=False
    )
```
